32 devices in a mesh: ctx: 8 (over z, x), tp: 4 (over y, core).
Axes of the slice: x: 2, y: 2, z: 4, core: 2. Of those that a mesh axis runs over, the one named last changes fastest.
Arguments:
- queries: bfloat16 [2048, 2048], P('ctx', 'tp'), may hold values from -6 to 6
- keys: bfloat16 [2048, 2048], P('ctx', 'tp'), may hold values from -6 to 6
- values: bfloat16 [2048, 2048], P('ctx', 'tp'), may hold values from -6 to 6
- out_grad: bfloat16 [2048, 4096], P('ctx', 'tp'), may hold values from -6 to 6
- w_out: bfloat16 [2048, 4096], P('tp'), may hold values from -0.09375 to 0.09375
- offsets: int32 [16, 3], P('tp'), may hold values from 0 to 3, as said below
Outputs:
- query_grad: bfloat16 [2048, 2048], P('ctx', 'tp')
- key_grad: bfloat16 [2048, 2048], P('ctx', 'tp')
- value_grad: bfloat16 [2048, 2048], P('ctx', 'tp')
The draws below stay inside these ranges and needn't reach their ends.
Inputs may be any that keep to these rules, and one draw needn't show every extreme that they name: offsets[h, l] lies between 0 and 2^l - 1.
All inputs are finite; a program needn't handle non-finite values.
Results may differ from the reference program's by a relative error of at most 0.017.
Values may be sent and summed in bfloat16 or wider, within the bound.
A program may use at most 64 MiB of HBM per device.

```python
import math
import jax
import jax.numpy as jnp
from jax import lax

D = 4096
HEADS = 16
HEAD_DIM = 128
LEVELS = 3
TOK_DEV = 256
TOKENS = 2048
KEYS_SEG = 1024


def draw_queries(key, part):
    drawn = jax.random.normal(jax.random.fold_in(key, 1), (TOKENS, HEADS * HEAD_DIM), jnp.float32)
    return jnp.clip(drawn, -6.0, 6.0).astype(jnp.bfloat16)


def draw_keys(key, part):
    drawn = jax.random.normal(jax.random.fold_in(key, 2), (TOKENS, HEADS * HEAD_DIM), jnp.float32)
    return jnp.clip(drawn, -6.0, 6.0).astype(jnp.bfloat16)


def draw_offsets(key, part):
    columns = []
    for level_num in range(LEVELS):
        order = jax.random.permutation(jax.random.fold_in(key, 11 + level_num), HEADS)
        columns.append(2 ** level_num - 1 - order * 2 ** level_num // HEADS)
    return jnp.stack(columns, axis=1).astype(jnp.int32)


def shard_levels(rng, extent, pieces, smallest, high):
    level, own = 1.0, jax.random.fold_in(rng, 6)
    for axis_at, parts in pieces:
        heights = jnp.exp(jax.random.uniform(jax.random.fold_in(own, axis_at), (parts,), jnp.float32, smallest / len(pieces), high / len(pieces)))
        level = level * jnp.repeat(heights, extent[axis_at] // parts).reshape([-1 if axis == axis_at else 1 for axis in range(len(extent))])
    return level


def scatter_about(key, shape, scale, bound, cuts=(), held_as=jnp.bfloat16):
    values = scale * jax.random.normal(key, shape, jnp.float32)
    if cuts:
        values = values * shard_levels(key, shape, cuts, -0.22, 0.18)
    return jnp.clip(values, -bound, bound).astype(held_as)


def setup_inputs(seed: int = 0) -> dict:
    seeds = jax.random.split(jax.random.key(seed), 7)
    queries = draw_queries(jax.random.fold_in(seeds[6], 71), 0)
    keys = draw_keys(jax.random.fold_in(seeds[6], 71), 0)
    values = scatter_about(seeds[2], (TOKENS, HEADS * HEAD_DIM), 1.0, 6.0, ((0, 8), (1, 4)))
    out_grad = scatter_about(seeds[3], (TOKENS, D), 1.0, 6.0, ((0, 8), (1, 4)))
    w_out = scatter_about(seeds[4], (HEADS * HEAD_DIM, D), D ** -0.5, 0.09375, ((0, 4),))
    offsets = draw_offsets(jax.random.fold_in(seeds[6], 71), 0)
    return dict(queries=queries, keys=keys, values=values, out_grad=out_grad, w_out=w_out, offsets=offsets)


NEGATIVE_FILL = -1e+30
HIGHEST_PRECISION = lax.Precision.HIGHEST

def low_round(values_in):
    return lax.optimization_barrier(values_in.astype(jnp.bfloat16)).astype(jnp.float32)

def reference(queries, keys, values, out_grad, w_out, offsets):
    score_scale = 1.0 / math.sqrt(HEAD_DIM)
    rotation = 2 * TOK_DEV
    grad_full = jnp.dot(out_grad, w_out.T, preferred_element_type=jnp.float32).astype(jnp.bfloat16)
    queries = jnp.roll(queries, -rotation, axis=0)
    keys = jnp.roll(keys, -rotation, axis=0)
    values = jnp.roll(values, -rotation, axis=0)
    grad_out = jnp.roll(grad_full, -rotation, axis=0)
    query_cols, key_cols, value_cols = ([], [], [])
    for head_num in range(HEADS):
        first_col = head_num * HEAD_DIM
        query_head = queries[:, first_col:first_col + HEAD_DIM].astype(jnp.float32)
        key_head = keys[:, first_col:first_col + HEAD_DIM].astype(jnp.float32)
        value_head = values[:, first_col:first_col + HEAD_DIM].astype(jnp.float32)
        grad_head = grad_out[:, first_col:first_col + HEAD_DIM].astype(jnp.float32)
        saved, tops, totals, sums = ([], [], [], [])
        for level_num in range(LEVELS):
            stride = 2 ** level_num
            seg_rows = min(KEYS_SEG, TOKENS // stride)
            causal = jnp.tril(jnp.ones((seg_rows, seg_rows), dtype=bool))
            positions = (offsets[head_num, level_num] + stride * jnp.arange(TOKENS // stride, dtype=jnp.int32)).astype(jnp.int32)
            query_pack = jnp.take(query_head, positions, axis=0).reshape(-1, seg_rows, HEAD_DIM)
            key_pack = jnp.take(key_head, positions, axis=0).reshape(-1, seg_rows, HEAD_DIM)
            value_pack = jnp.take(value_head, positions, axis=0).reshape(-1, seg_rows, HEAD_DIM)
            grad_pack = jnp.take(grad_head, positions, axis=0).reshape(-1, seg_rows, HEAD_DIM)
            scores = jnp.einsum('sad,sbd->sab', query_pack, key_pack, precision=HIGHEST_PRECISION) * score_scale
            scores = jnp.where(causal, scores, NEGATIVE_FILL)
            row_top = lax.optimization_barrier(jnp.max(scores, axis=2))
            weights = jnp.where(causal, jnp.exp(scores - row_top[:, :, None]), 0.0)
            level_sum = jnp.einsum('sab,sbd->sad', weights, value_pack, precision=HIGHEST_PRECISION)
            tops.append(jnp.full((TOKENS,), NEGATIVE_FILL, jnp.float32).at[positions].set(row_top.reshape(-1)))
            totals.append(jnp.zeros((TOKENS,), jnp.float32).at[positions].set(lax.optimization_barrier(jnp.sum(weights, axis=2)).reshape(-1)))
            sums.append(jnp.zeros((TOKENS, HEAD_DIM), jnp.float32).at[positions].set(level_sum.reshape(-1, HEAD_DIM)))
            saved.append((positions, causal, seg_rows, scores, query_pack, key_pack, value_pack, grad_pack))
        row_top = tops[0]
        for level_top in tops[1:]:
            row_top = jnp.maximum(row_top, level_top)
        row_total = jnp.zeros((TOKENS,), jnp.float32)
        out_sum = jnp.zeros((TOKENS, HEAD_DIM), jnp.float32)
        for level_top, level_total, level_sum in zip(tops, totals, sums):
            factor = jnp.exp(level_top - row_top)
            row_total = row_total + level_total * factor
            out_sum = out_sum + level_sum * factor[:, None]
        log_total = row_top + jnp.log(row_total)
        attn_out = out_sum / row_total[:, None]
        delta = lax.optimization_barrier(jnp.sum(grad_head * attn_out, axis=1))
        query_grad = jnp.zeros((TOKENS, HEAD_DIM), jnp.float32)
        key_grad = jnp.zeros((TOKENS, HEAD_DIM), jnp.float32)
        value_grad = jnp.zeros((TOKENS, HEAD_DIM), jnp.float32)
        for positions, causal, seg_rows, scores, query_pack, key_pack, value_pack, grad_pack in saved:
            log_pack = jnp.take(log_total, positions).reshape(-1, seg_rows)
            delta_pack = jnp.take(delta, positions).reshape(-1, seg_rows)
            weight = jnp.where(causal, jnp.exp(scores - log_pack[:, :, None]), 0.0)
            prob_grad = jnp.einsum('sad,sbd->sab', grad_pack, value_pack, precision=HIGHEST_PRECISION)
            score_grad = low_round(weight * (prob_grad - delta_pack[:, :, None]))
            weight_low = low_round(weight)
            query_grad = query_grad.at[positions].add(jnp.einsum('sab,sbd->sad', score_grad, key_pack, precision=HIGHEST_PRECISION).reshape(-1, HEAD_DIM))
            key_grad = key_grad.at[positions].add(jnp.einsum('sab,sad->sbd', score_grad, query_pack, precision=HIGHEST_PRECISION).reshape(-1, HEAD_DIM))
            value_grad = value_grad.at[positions].add(jnp.einsum('sab,sad->sbd', weight_low, grad_pack, precision=HIGHEST_PRECISION).reshape(-1, HEAD_DIM))
        query_cols.append(jnp.roll((query_grad * score_scale).astype(jnp.bfloat16), rotation, axis=0))
        key_cols.append(jnp.roll((key_grad * score_scale).astype(jnp.bfloat16), rotation, axis=0))
        value_cols.append(jnp.roll(value_grad.astype(jnp.bfloat16), rotation, axis=0))
    return (jnp.concatenate(query_cols, axis=1), jnp.concatenate(key_cols, axis=1), jnp.concatenate(value_cols, axis=1))
```

```python
import functools
import math

import jax
import jax.numpy as jnp
from jax import lax
from jax.experimental import pallas as pl
from jax.experimental.pallas import tpu as pltpu
from jax.sharding import PartitionSpec as P

LEVELS = 3
KEYS_SEG = 1024
MESH = pl.DeviceIdType.MESH
NEGATIVE_FILL = -1e30
CHUNKS = 4
SUB = 128
F32 = jnp.float32
BF16 = jnp.bfloat16


def nt(a, b):
    return lax.dot_general(a, b, (((1,), (1,)), ((), ())), preferred_element_type=F32)


def tn(a, b):
    return lax.dot_general(a, b, (((0,), (0,)), ((), ())), preferred_element_type=F32)


def kernel(
    n, q_ref, k_ref, v_ref, og_ref, w_hbm, off_ref, dq_ref, dk_ref, dv_ref,
    w_buf, og_buf, grad_buf, q_buf, g_buf, kv_buf, s_buf, p_buf, ds_buf, wl_buf,
    dkv_acc, dkv_low, dq_low, part_buf,
    w_sem, og_send, og_recv, fw_send, fw_recv, pair_send, pair_recv,
    kv_send, kv_recv, q_send, q_recv, g_send, g_recv,
    dq_send, dq_recv, part_send, part_recv,
):
    tok, width = q_ref.shape
    heads = off_ref.shape[0]
    dim = width // heads
    feats = og_ref.shape[1]
    group = min(KEYS_SEG * 2 ** (LEVELS - 1), tok * n) // tok
    pairs = group // 2
    rows = 2 * tok
    quads = n // 4
    turns = group // 4
    wide = n > group
    me = lax.axis_index("ctx")
    tp = lax.axis_index("tp")
    quad, head = me // 4, me % 4
    start = (4 * quad) % group
    straddle = start == 0
    u_block = (me + n - 2) % n
    own_group, own_slot = u_block // group, u_block % group
    first_group = ((4 * quad + n - 2) % n) // group
    core_peer = tp + 1 - 2 * (tp % 2)
    y_peer = (tp + 2) % 4
    far_peer = (core_peer + 2) % 4

    def move(src, dst, send, recv, target):
        @pl.when(target != me)
        def _():
            pltpu.make_async_remote_copy(
                src_ref=src, dst_ref=dst, send_sem=send, recv_sem=recv,
                device_id={"ctx": target}, device_id_type=MESH,
            ).start()

        @pl.when(target == me)
        def _():
            pltpu.make_async_copy(src, dst, recv).start()

    def sent(src, send, target):
        @pl.when(target != me)
        def _():
            pltpu.make_async_copy(src, src, send).wait()

    def arrived(dst, recv):
        pltpu.make_async_copy(dst, dst, recv).wait()

    def cols(index):
        return pl.ds(pl.multiple_of(index * dim, dim), dim)

    def block(index, size):
        return pl.ds(pl.multiple_of(index * size, size), size)

    w_copy = pltpu.make_async_copy(w_hbm, w_buf, w_sem)
    w_copy.start()

    barrier = pltpu.get_barrier_semaphore()
    for step in range(1, n):
        pl.semaphore_signal(
            barrier, inc=1, device_id={"ctx": (me + step) % n}, device_id_type=MESH
        )
    for peer in (core_peer, y_peer):
        pl.semaphore_signal(barrier, inc=1, device_id={"tp": peer}, device_id_type=MESH)
    pl.semaphore_wait(barrier, n + 1)

    def tp_copy(src, dst, send, recv, peer):
        return pltpu.make_async_remote_copy(
            src_ref=src, dst_ref=dst, send_sem=send, recv_sem=recv,
            device_id={"tp": peer}, device_id_type=MESH,
        )

    piece = feats // CHUNKS
    for c in range(CHUNKS):
        part = pl.ds(c * piece, piece)
        tp_copy(
            og_ref.at[:, part], og_buf.at[1, :, part], og_send.at[c], og_recv.at[c], y_peer
        ).start()
    tp_copy(og_ref, og_buf.at[0], pair_send, pair_recv, core_peer).start()

    sources = (k_ref, v_ref)

    def turn_list():
        listed = []
        for j in range(1, turns + 1):
            needed = own_slot <= 4 * j + 1
            listed.append((j, j - 1, needed, own_slot))
        if wide:
            listed.append((0, turns, own_slot < 2, group + own_slot))
        return listed

    def each_kv(act):
        for j, at, needed, slot in turn_list():
            @pl.when(needed)
            def _(j=j, at=at, slot=slot):
                to_quad = (own_group * turns + j) % quads
                for h in range(4):
                    for kind in range(2):
                        act(kind, at, h, slot, 4 * to_quad + h)

    for h in range(4):
        move(
            q_ref.at[:, pl.ds(h * dim, dim)], q_buf.at[block(head, tok)],
            q_send.at[h], q_recv.at[head], 4 * quad + h,
        )
    each_kv(
        lambda kind, at, h, slot, target: move(
            sources[kind].at[:, pl.ds(h * dim, dim)], kv_buf.at[kind, block(slot, tok)],
            kv_send.at[kind, at, h], kv_recv.at[kind, slot], target,
        )
    )

    dkv_acc[...] = jnp.zeros_like(dkv_acc)

    w_copy.wait()

    def w_part(shard, c):
        return w_buf[:, pl.ds(pl.multiple_of(shard * feats + c * piece, piece), piece)]

    total = nt(og_ref[...], w_buf[:, block(tp, feats)])
    arrived(og_buf.at[0], pair_recv)
    total += nt(og_buf[0], w_buf[:, block(core_peer, feats)])
    for c in range(CHUNKS):
        part = pl.ds(c * piece, piece)
        arrived(og_buf.at[1, :, part], og_recv.at[c])
        tp_copy(
            og_buf.at[1, :, part], og_buf.at[2, :, part], fw_send.at[c], fw_recv.at[c], core_peer
        ).start()
        total += nt(og_buf[1, :, part], w_part(y_peer, c))
    for c in range(CHUNKS):
        part = pl.ds(c * piece, piece)
        arrived(og_buf.at[2, :, part], fw_recv.at[c])
        total += nt(og_buf[2, :, part], w_part(far_peer, c))
    grad_buf[...] = total.astype(BF16)
    for h in range(4):
        move(
            grad_buf.at[:, pl.ds(h * dim, dim)], g_buf.at[block(head, tok)],
            g_send.at[h], g_recv.at[head], 4 * quad + h,
        )

    def slot_needed(slot):
        return straddle | (slot <= start + 1)

    def each_slot(act):
        for slot in range(group):
            pl.when(slot_needed(slot))(functools.partial(act, slot))
        if wide:
            for slot in range(group, group + 2):
                pl.when(straddle)(functools.partial(act, slot))

    def wait_kind(kind):
        each_slot(lambda slot: arrived(kv_buf.at[kind, block(slot, tok)], kv_recv.at[kind, slot]))

    for b in range(4):
        arrived(q_buf.at[block(b, tok)], q_recv.at[b])
    wait_kind(0)

    odd1, odd2 = off_ref[head, 1], off_ref[head, 2]
    key_row = lax.broadcasted_iota(jnp.int32, (8, rows), 0)
    query_col = lax.broadcasted_iota(jnp.int32, (8, rows), 1)
    both1 = ((key_row % 2 == odd1) & (query_col % 2 == odd1)).astype(F32)
    both2 = ((key_row % 4 == odd2) & (query_col % 4 == odd2)).astype(F32)
    sub_row = lax.broadcasted_iota(jnp.int32, (SUB, rows), 0)
    sub_col = lax.broadcasted_iota(jnp.int32, (SUB, rows), 1)
    score_scale = 1.0 / math.sqrt(dim)
    to_exp2 = score_scale / math.log(2.0)
    halves = []
    for half in range(2):
        if half == 0:
            at_pair = jnp.where(straddle, pairs - 1, start // 2 - 1)
            base = 0
        else:
            at_pair = jnp.where(straddle, 0, start // 2)
            base = jnp.where(straddle, pairs, 0) if wide else 0
        halves.append((at_pair, base))

    def folded(values):
        return values.reshape(values.shape[0] // 8, 8, values.shape[1])

    tops = []
    for half, (at_pair, base) in enumerate(halves):
        queries = q_buf[half * rows:(half + 1) * rows, :]

        def score_body(kp, top, half=half, at_pair=at_pair, base=base, queries=queries):
            same0 = jnp.where(at_pair // 2 == kp // 2, 1.0, 0.0)
            same1 = jnp.where(at_pair // 4 == kp // 4, 1.0, 0.0)
            count = same0 + same1 * both1 + both2
            bias = jnp.where(
                count > 2.5, math.log2(3.0),
                jnp.where(count > 1.5, 1.0, jnp.where(count > 0.5, 0.0, NEGATIVE_FILL)),
            )
            lead = (at_pair - kp) * rows
            for s in range(rows // SUB):
                keys = kv_buf[0, pl.ds(pl.multiple_of((base + kp) * rows + s * SUB, SUB), SUB), :]
                scores = folded(nt(keys, queries) * to_exp2) + bias[None]
                scores = scores.reshape(SUB, rows)
                scores = jnp.where(sub_row + s * SUB <= sub_col + lead, scores, NEGATIVE_FILL)
                s_buf[half, kp, s * SUB:(s + 1) * SUB, :] = scores
                top = jnp.maximum(top, jnp.max(folded(scores), axis=0))
            return top

        top = lax.fori_loop(
            0, at_pair + 1, score_body, jnp.full((8, rows), NEGATIVE_FILL, F32)
        )
        tops.append(jnp.max(top, axis=0, keepdims=True))

    wait_kind(1)
    for b in range(4):
        arrived(g_buf.at[block(b, tok)], g_recv.at[b])

    part_at = jnp.where(straddle, turns, start // 4) - 1

    def slot_owner(slot):
        return (first_group * group + slot + 2) % n

    def send_slot(slot, owner, at):
        for kind in range(2):
            move(
                dkv_low.at[kind, block(slot, tok)], part_buf.at[kind, at, :, cols(head)],
                part_send.at[kind, slot], part_recv.at[kind, at, head], owner,
            )

    def round_pair(kp):
        dkv_low[0, block(kp, rows), :] = (dkv_acc[0, block(kp, rows), :] * score_scale).astype(BF16)
        dkv_low[1, block(kp, rows), :] = dkv_acc[1, block(kp, rows), :].astype(BF16)

    def send_pair(kp):
        round_pair(kp)
        for b in range(2):
            slot = 2 * kp + b
            send_slot(slot, slot_owner(slot), part_at)

    shared = jnp.where(straddle, 0, halves[1][0] + 1) if wide else halves[1][0] + 1

    for half, (at_pair, base) in enumerate(halves):
        queries = q_buf[half * rows:(half + 1) * rows, :]
        grads = g_buf[half * rows:(half + 1) * rows, :]
        top = tops[half]

        def weigh_body(kp, sums, half=half, base=base, grads=grads, top=top):
            den, num = sums
            for s in range(rows // SUB):
                here = slice(s * SUB, (s + 1) * SUB)
                vals = kv_buf[1, pl.ds(pl.multiple_of((base + kp) * rows + s * SUB, SUB), SUB), :]
                prob = nt(vals, grads)
                weight = jnp.exp2(s_buf[half, kp, here, :] - top)
                s_buf[half, kp, here, :] = weight
                p_buf[kp, here, :] = prob
                den = den + jnp.sum(folded(weight), axis=0)
                num = num + jnp.sum(folded(weight * prob), axis=0)
            return den, num

        zero = jnp.zeros((8, rows), F32)
        den, num = lax.fori_loop(0, at_pair + 1, weigh_body, (zero, zero))
        inverse = 1.0 / jnp.sum(den, axis=0, keepdims=True)
        delta = jnp.sum(num, axis=0, keepdims=True) * inverse

        def grad_body(
            kp, total, half=half, base=base, queries=queries, grads=grads,
            inverse=inverse, delta=delta,
        ):
            for s in range(rows // SUB):
                here = slice(s * SUB, (s + 1) * SUB)
                weight = s_buf[half, kp, here, :] * inverse
                wl_buf[here, :] = weight.astype(BF16)
                ds_buf[here, :] = (weight * (p_buf[kp, here, :] - delta)).astype(BF16)
            place = block(base + kp, rows)
            score_grad = ds_buf[...]
            dkv_acc[0, place, :] += jnp.dot(score_grad, queries, preferred_element_type=F32)
            dkv_acc[1, place, :] += jnp.dot(wl_buf[...], grads, preferred_element_type=F32)
            total = total + tn(kv_buf[0, place, :], score_grad)
            if half == 1:
                if wide:
                    pl.when(jnp.logical_not(straddle))(functools.partial(send_pair, kp))
                else:
                    send_pair(kp)
            return total

        total = lax.fori_loop(0, at_pair + 1, grad_body, jnp.zeros((dim, rows), F32))
        dq_low[half * rows:(half + 1) * rows, :] = (total * score_scale).T.astype(BF16)
        for b in range(2 * half, 2 * half + 2):
            move(
                dq_low.at[pl.ds(b * tok, tok)], dq_ref.at[:, cols(head)],
                dq_send.at[b], dq_recv.at[head], 4 * quad + b,
            )
        if half == 0:
            lax.fori_loop(shared, at_pair + 1, lambda kp, none: (send_pair(kp), none)[1], 0)
    if wide:
        @pl.when(straddle)
        def _():
            round_pair(pairs)
            for b in range(2):
                send_slot(group + b, (4 * quad + b + 2) % n, turns)

    for j, at, needed, slot in turn_list():
        @pl.when(needed)
        def _(at=at):
            for kind in range(2):
                for h in range(4):
                    arrived(part_buf.at[kind, at, :, pl.ds(h * dim, dim)], part_recv.at[kind, at, h])
    for kind, out in ((0, dk_ref), (1, dv_ref)):
        dkv_sum = part_buf[kind, turns - 1].astype(F32)
        for j, at, needed, slot in turn_list():
            if at != turns - 1:
                dkv_sum = dkv_sum + jnp.where(needed, part_buf[kind, at].astype(F32), 0.0)
        out[...] = dkv_sum.astype(BF16)
    for h in range(4):
        arrived(dq_ref.at[:, pl.ds(h * dim, dim)], dq_recv.at[h])

    for c in range(CHUNKS):
        part = pl.ds(c * piece, piece)
        pltpu.make_async_copy(og_ref.at[:, part], og_ref.at[:, part], og_send.at[c]).wait()
        pltpu.make_async_copy(og_ref.at[:, part], og_ref.at[:, part], fw_send.at[c]).wait()
    pltpu.make_async_copy(og_ref, og_ref, pair_send).wait()
    for h in range(4):
        sent(q_ref.at[:, pl.ds(h * dim, dim)], q_send.at[h], 4 * quad + h)
        sent(grad_buf.at[:, pl.ds(h * dim, dim)], g_send.at[h], 4 * quad + h)
        sent(dq_low.at[pl.ds(h * tok, tok)], dq_send.at[h], 4 * quad + h)
    each_kv(
        lambda kind, at, h, slot, target: sent(
            sources[kind].at[:, pl.ds(h * dim, dim)], kv_send.at[kind, at, h], target
        )
    )

    def slot_sent(slot):
        owner = slot_owner(slot) if slot < group else (4 * quad + slot - group + 2) % n
        for kind in range(2):
            sent(dkv_low.at[kind, pl.ds(slot * tok, tok)], part_send.at[kind, slot], owner)

    each_slot(slot_sent)


def local(queries, keys, values, out_grad, w_out, offsets):
    n = lax.axis_size("ctx")
    tok, width = queries.shape
    heads = offsets.shape[0]
    dim = width // heads
    feats = out_grad.shape[1]
    group = min(KEYS_SEG * 2 ** (LEVELS - 1), tok * n) // tok
    assert heads == 4 and tok * 4 == KEYS_SEG and lax.axis_size("tp") == 4
    assert n % group == 0 and group % 4 == 0
    pairs, rows, turns = group // 2, 2 * tok, group // 4
    wide = n > group
    slots = group + 2 * wide
    kinds = turns + wide
    dma = pltpu.SemaphoreType.DMA
    vmem = pl.BlockSpec(memory_space=pltpu.VMEM)
    out = jax.ShapeDtypeStruct((tok, width), BF16)
    return pl.pallas_call(
        functools.partial(kernel, n),
        out_shape=(out, out, out),
        in_specs=[vmem, vmem, vmem, vmem, pl.BlockSpec(memory_space=pl.ANY),
                  pl.BlockSpec(memory_space=pltpu.SMEM)],
        out_specs=(vmem, vmem, vmem),
        scratch_shapes=[
            pltpu.VMEM(w_out.shape, BF16),
            pltpu.VMEM((3, tok, feats), BF16),
            pltpu.VMEM((tok, width), BF16),
            pltpu.VMEM((4 * tok, dim), BF16),
            pltpu.VMEM((4 * tok, dim), BF16),
            pltpu.VMEM((2, slots * tok, dim), BF16),
            pltpu.VMEM((2, pairs, rows, rows), F32),
            pltpu.VMEM((pairs, rows, rows), F32),
            pltpu.VMEM((rows, rows), BF16),
            pltpu.VMEM((rows, rows), BF16),
            pltpu.VMEM((2, slots * tok, dim), F32),
            pltpu.VMEM((2, slots * tok, dim), BF16),
            pltpu.VMEM((4 * tok, dim), BF16),
            pltpu.VMEM((2, kinds, tok, width), BF16),
            dma, dma((CHUNKS,)), dma((CHUNKS,)), dma((CHUNKS,)), dma((CHUNKS,)), dma, dma,
            dma((2, kinds, 4)), dma((2, slots)), dma((4,)), dma((4,)), dma((4,)), dma((4,)),
            dma((4,)), dma((4,)), dma((2, slots)), dma((2, kinds, 4)),
        ],
        compiler_params=pltpu.CompilerParams(
            collective_id=0, has_side_effects=True, vmem_limit_bytes=56 * 1024 * 1024
        ),
        cost_estimate=pl.CostEstimate(
            flops=5 * 10 * rows * rows * dim + 2 * tok * width * feats * 4,
            bytes_accessed=2 * (w_out.size + 8 * tok * width), transcendentals=5 * rows * rows,
        ),
    )(queries, keys, values, out_grad, w_out, offsets)


def solution(mesh):
    return jax.shard_map(
        local,
        mesh=mesh,
        in_specs=(
            P("ctx", "tp"),
            P("ctx", "tp"),
            P("ctx", "tp"),
            P("ctx", "tp"),
            P("tp", None),
            P("tp", None),
        ),
        out_specs=(P("ctx", "tp"), P("ctx", "tp"), P("ctx", "tp")),
        check_vma=False,
    )
```

```python
import functools
import math

import jax
import jax.numpy as jnp
from jax import lax
from jax.experimental import pallas as pl
from jax.experimental.pallas import tpu as pltpu
from jax.sharding import PartitionSpec as P

LEVELS = 3
KEYS_SEG = 1024
MESH = pl.DeviceIdType.MESH
NEGATIVE_FILL = -1e30
CHUNKS = 4
SUB = 128
F32 = jnp.float32
BF16 = jnp.bfloat16


def nt(a, b):
    return lax.dot_general(a, b, (((1,), (1,)), ((), ())), preferred_element_type=F32)


def tn(a, b):
    return lax.dot_general(a, b, (((0,), (0,)), ((), ())), preferred_element_type=F32)


def owner_turns(group, wide, own_slot):
    turns = group // 4
    listed = [(turns, turns - 1, own_slot < group, own_slot)]
    for j in range(1, turns):
        listed.append((j, j - 1, own_slot <= 4 * j + 1, own_slot))
    if wide:
        listed.append((0, turns, own_slot < 2, group + own_slot))
    return listed


def kernel(
    n, q_ref, k_ref, v_ref, og_ref, w_hbm, off_ref, dq_ref, part_buf,
    w_buf, og_buf, grad_buf, q_buf, g_buf, kv_buf, s_buf, p_buf, ds_buf, wl_buf,
    dkv_acc, dkv_low, dq_low,
    w_sem, og_sem, og_send, og_recv, fw_send, fw_recv, pair_send, pair_recv,
    kv_send, kv_recv, q_send, q_recv, g_send, g_recv,
    dq_send, dq_recv, part_send, part_recv,
):
    tok, width = q_ref.shape
    heads = off_ref.shape[0]
    dim = width // heads
    feats = og_ref.shape[1]
    group = min(KEYS_SEG * 2 ** (LEVELS - 1), tok * n) // tok
    pairs = group // 2
    rows = 2 * tok
    quads = n // 4
    turns = group // 4
    wide = n > group
    me = lax.axis_index("ctx")
    tp = lax.axis_index("tp")
    quad, head = me // 4, me % 4
    start = (4 * quad) % group
    straddle = start == 0
    u_block = (me + n - 2) % n
    own_group, own_slot = u_block // group, u_block % group
    first_group = ((4 * quad + n - 2) % n) // group
    core_peer = tp + 1 - 2 * (tp % 2)
    y_peer = (tp + 2) % 4
    far_peer = (core_peer + 2) % 4

    def move(src, dst, send, recv, target):
        @pl.when(target != me)
        def _():
            pltpu.make_async_remote_copy(
                src_ref=src, dst_ref=dst, send_sem=send, recv_sem=recv,
                device_id={"ctx": target}, device_id_type=MESH,
            ).start()

        @pl.when(target == me)
        def _():
            pltpu.make_async_copy(src, dst, recv).start()

    def sent(src, send, target):
        @pl.when(target != me)
        def _():
            pltpu.make_async_copy(src, src, send).wait()

    def arrived(dst, recv):
        pltpu.make_async_copy(dst, dst, recv).wait()

    def cols(index):
        return pl.ds(pl.multiple_of(index * dim, dim), dim)

    def block(index, size):
        return pl.ds(pl.multiple_of(index * size, size), size)

    w_copy = pltpu.make_async_copy(w_hbm, w_buf, w_sem)
    w_copy.start()
    og_copy = pltpu.make_async_copy(og_ref, og_buf.at[3], og_sem)
    og_copy.start()

    barrier = pltpu.get_barrier_semaphore()
    for step in range(1, n):
        pl.semaphore_signal(
            barrier, inc=1, device_id={"ctx": (me + step) % n}, device_id_type=MESH
        )
    for peer in (core_peer, y_peer):
        pl.semaphore_signal(barrier, inc=1, device_id={"tp": peer}, device_id_type=MESH)
    pl.semaphore_wait(barrier, n + 1)

    def tp_copy(src, dst, send, recv, peer):
        return pltpu.make_async_remote_copy(
            src_ref=src, dst_ref=dst, send_sem=send, recv_sem=recv,
            device_id={"tp": peer}, device_id_type=MESH,
        )

    piece = feats // CHUNKS
    for c in range(CHUNKS):
        part = pl.ds(c * piece, piece)
        tp_copy(
            og_ref.at[:, part], og_buf.at[1, :, part], og_send.at[c], og_recv.at[c], y_peer
        ).start()
    tp_copy(og_ref, og_buf.at[0], pair_send, pair_recv, core_peer).start()

    sources = (k_ref, v_ref)
    turn_list = owner_turns(group, wide, own_slot)

    def send_kv(act, kind, entry):
        j, at, needed, slot = entry

        @pl.when(needed)
        def _():
            to_quad = (own_group * turns + j) % quads
            for h in range(4):
                act(kind, at, h, slot, 4 * to_quad + h)

    def start_kv(kind, at, h, slot, target):
        move(
            sources[kind].at[:, pl.ds(h * dim, dim)], kv_buf.at[kind, block(slot, tok)],
            kv_send.at[kind, at, h], kv_recv.at[kind, slot], target,
        )

    send_kv(start_kv, 0, turn_list[0])
    for h in range(4):
        move(
            q_ref.at[:, pl.ds(h * dim, dim)], q_buf.at[block(head, tok)],
            q_send.at[h], q_recv.at[head], 4 * quad + h,
        )
    send_kv(start_kv, 1, turn_list[0])
    for kind in range(2):
        for entry in turn_list[1:]:
            send_kv(start_kv, kind, entry)

    dkv_acc[...] = jnp.zeros_like(dkv_acc)

    w_copy.wait()
    og_copy.wait()

    def w_part(shard, c):
        return w_buf[:, pl.ds(pl.multiple_of(shard * feats + c * piece, piece), piece)]

    total = nt(og_buf[3], w_buf[:, block(tp, feats)])
    arrived(og_buf.at[0], pair_recv)
    total += nt(og_buf[0], w_buf[:, block(core_peer, feats)])
    for c in range(CHUNKS):
        part = pl.ds(c * piece, piece)
        arrived(og_buf.at[1, :, part], og_recv.at[c])
        tp_copy(
            og_buf.at[1, :, part], og_buf.at[2, :, part], fw_send.at[c], fw_recv.at[c], core_peer
        ).start()
        total += nt(og_buf[1, :, part], w_part(y_peer, c))
    for c in range(CHUNKS):
        part = pl.ds(c * piece, piece)
        arrived(og_buf.at[2, :, part], fw_recv.at[c])
        total += nt(og_buf[2, :, part], w_part(far_peer, c))
    grad_buf[...] = total.astype(BF16)
    for h in range(4):
        move(
            grad_buf.at[:, pl.ds(h * dim, dim)], g_buf.at[block(head, tok)],
            g_send.at[h], g_recv.at[head], 4 * quad + h,
        )

    def wait_pair(kind, pair):
        for b in range(2):
            slot = 2 * pair + b
            arrived(kv_buf.at[kind, block(slot, tok)], kv_recv.at[kind, slot])

    for b in range(4):
        arrived(q_buf.at[block(b, tok)], q_recv.at[b])

    odd1, odd2 = off_ref[head, 1], off_ref[head, 2]
    key_row = lax.broadcasted_iota(jnp.int32, (8, rows), 0)
    query_col = lax.broadcasted_iota(jnp.int32, (8, rows), 1)
    both1 = ((key_row % 2 == odd1) & (query_col % 2 == odd1)).astype(F32)
    both2 = ((key_row % 4 == odd2) & (query_col % 4 == odd2)).astype(F32)
    sub_row = lax.broadcasted_iota(jnp.int32, (SUB, rows), 0)
    sub_col = lax.broadcasted_iota(jnp.int32, (SUB, rows), 1)
    score_scale = 1.0 / math.sqrt(dim)
    to_exp2 = score_scale / math.log(2.0)
    first_pair = jnp.where(straddle, 0, start // 2 - 1)
    first_base = jnp.where(straddle, pairs, 0) if wide else 0
    last_pair = jnp.where(straddle, pairs - 1, start // 2)
    early = jnp.where(straddle, 1, 0)
    halves = [(early, first_pair, first_base), (1 - early, last_pair, 0)]

    def arrival(turn, step):
        count = halves[turn][1] + 1
        return step if turn == 0 else (step + jnp.where(straddle, count - 1, 1)) % count

    def wait_new(turn, kind, kp):
        if turn == 0:
            wait_pair(kind, first_base + kp)
        else:
            fresh = kp > first_pair
            if wide:
                fresh = fresh | straddle
            pl.when(fresh)(functools.partial(wait_pair, kind, kp))

    def folded(values):
        return values.reshape(values.shape[0] // 8, 8, values.shape[1])

    tops = []
    for turn, (half, at_pair, base) in enumerate(halves):
        queries = q_buf[block(half, rows), :]

        def score_body(step, top, turn=turn, at_pair=at_pair, base=base, queries=queries):
            kp = arrival(turn, step)
            wait_new(turn, 0, kp)
            same0 = jnp.where(at_pair // 2 == kp // 2, 1.0, 0.0)
            same1 = jnp.where(at_pair // 4 == kp // 4, 1.0, 0.0)
            count = same0 + same1 * both1 + both2
            bias = jnp.where(
                count > 2.5, math.log2(3.0),
                jnp.where(count > 1.5, 1.0, jnp.where(count > 0.5, 0.0, NEGATIVE_FILL)),
            )
            lead = (at_pair - kp) * rows
            for s in range(rows // SUB):
                keys = kv_buf[0, pl.ds(pl.multiple_of((base + kp) * rows + s * SUB, SUB), SUB), :]
                scores = folded(nt(keys, queries) * to_exp2) + bias[None]
                scores = scores.reshape(SUB, rows)
                scores = jnp.where(sub_row + s * SUB <= sub_col + lead, scores, NEGATIVE_FILL)
                s_buf[turn, kp, s * SUB:(s + 1) * SUB, :] = scores
                top = jnp.maximum(top, jnp.max(folded(scores), axis=0))
            return top

        top = lax.fori_loop(
            0, at_pair + 1, score_body, jnp.full((8, rows), NEGATIVE_FILL, F32)
        )
        tops.append(jnp.max(top, axis=0, keepdims=True))

    part_at = jnp.where(straddle, turns, start // 4) - 1

    def slot_owner(slot):
        return (first_group * group + slot + 2) % n

    def send_slot(slot, owner, at):
        for kind in range(2):
            move(
                dkv_low.at[kind, block(slot, tok)], part_buf.at[kind, at, :, cols(head)],
                part_send.at[kind, slot], part_recv.at[kind, at, head], owner,
            )

    def round_pair(kp):
        dkv_low[0, block(kp, rows), :] = (dkv_acc[0, block(kp, rows), :] * score_scale).astype(BF16)
        dkv_low[1, block(kp, rows), :] = dkv_acc[1, block(kp, rows), :].astype(BF16)

    def send_pair(kp):
        round_pair(kp)
        for b in range(2):
            slot = 2 * kp + b
            send_slot(slot, slot_owner(slot), part_at)

    for turn, (half, at_pair, base) in enumerate(halves):
        queries = q_buf[block(half, rows), :]
        for b in range(2):
            arrived(g_buf.at[block(2 * half + b, tok)], g_recv.at[2 * half + b])
        grads = g_buf[block(half, rows), :]
        top = tops[turn]

        def weigh_body(step, sums, turn=turn, base=base, grads=grads, top=top):
            kp = arrival(turn, step)
            wait_new(turn, 1, kp)
            den, num = sums
            for s in range(rows // SUB):
                here = slice(s * SUB, (s + 1) * SUB)
                vals = kv_buf[1, pl.ds(pl.multiple_of((base + kp) * rows + s * SUB, SUB), SUB), :]
                prob = nt(vals, grads)
                weight = jnp.exp2(s_buf[turn, kp, here, :] - top)
                s_buf[turn, kp, here, :] = weight
                p_buf[kp, here, :] = prob
                den = den + jnp.sum(folded(weight), axis=0)
                num = num + jnp.sum(folded(weight * prob), axis=0)
            return den, num

        zero = jnp.zeros((8, rows), F32)
        den, num = lax.fori_loop(0, at_pair + 1, weigh_body, (zero, zero))
        inverse = 1.0 / jnp.sum(den, axis=0, keepdims=True)
        delta = jnp.sum(num, axis=0, keepdims=True) * inverse

        def grad_body(
            step, total, turn=turn, at_pair=at_pair, base=base, queries=queries, grads=grads,
            inverse=inverse, delta=delta,
        ):
            kp = step
            if turn == 1:
                kp = (step + jnp.where(straddle, 1, 0)) % (at_pair + 1)
            for s in range(rows // SUB):
                here = slice(s * SUB, (s + 1) * SUB)
                weight = s_buf[turn, kp, here, :] * inverse
                wl_buf[here, :] = weight.astype(BF16)
                ds_buf[here, :] = (weight * (p_buf[kp, here, :] - delta)).astype(BF16)
            place = block(base + kp, rows)
            score_grad = ds_buf[...]
            dkv_acc[0, place, :] += jnp.dot(score_grad, queries, preferred_element_type=F32)
            dkv_acc[1, place, :] += jnp.dot(wl_buf[...], grads, preferred_element_type=F32)
            total = total + tn(kv_buf[0, place, :], score_grad)
            if turn == 1:
                send_pair(kp)
            return total

        total = lax.fori_loop(0, at_pair + 1, grad_body, jnp.zeros((dim, rows), F32))
        dq_low[block(half, rows), :] = (total * score_scale).T.astype(BF16)
        for b in range(2):
            move(
                dq_low.at[block(2 * half + b, tok)], dq_ref.at[:, cols(head)],
                dq_send.at[2 * half + b], dq_recv.at[head], 4 * quad + 2 * half + b,
            )
    if wide:
        @pl.when(straddle)
        def _():
            round_pair(pairs)
            for b in range(2):
                send_slot(group + b, (4 * quad + b + 2) % n, turns)

    for j, at, needed, slot in turn_list:
        @pl.when(needed)
        def _(at=at):
            for kind in range(2):
                for h in range(4):
                    arrived(part_buf.at[kind, at, :, pl.ds(h * dim, dim)], part_recv.at[kind, at, h])
    for h in range(4):
        arrived(dq_ref.at[:, pl.ds(h * dim, dim)], dq_recv.at[h])

    for c in range(CHUNKS):
        part = pl.ds(c * piece, piece)
        pltpu.make_async_copy(og_ref.at[:, part], og_ref.at[:, part], og_send.at[c]).wait()
        pltpu.make_async_copy(og_ref.at[:, part], og_ref.at[:, part], fw_send.at[c]).wait()
    pltpu.make_async_copy(og_ref, og_ref, pair_send).wait()
    for h in range(4):
        sent(q_ref.at[:, pl.ds(h * dim, dim)], q_send.at[h], 4 * quad + h)
        sent(grad_buf.at[:, pl.ds(h * dim, dim)], g_send.at[h], 4 * quad + h)
        sent(dq_low.at[pl.ds(h * tok, tok)], dq_send.at[h], 4 * quad + h)

    def kv_sent(kind, at, h, slot, target):
        sent(sources[kind].at[:, pl.ds(h * dim, dim)], kv_send.at[kind, at, h], target)

    for kind in range(2):
        for entry in turn_list:
            send_kv(kv_sent, kind, entry)

    def slot_sent(slot):
        owner = slot_owner(slot) if slot < group else (4 * quad + slot - group + 2) % n
        for kind in range(2):
            sent(dkv_low.at[kind, pl.ds(slot * tok, tok)], part_send.at[kind, slot], owner)

    for slot in range(group + 2 * wide):
        needed = straddle | (slot <= start + 1) if slot < group else straddle
        pl.when(needed)(functools.partial(slot_sent, slot))


def add_kernel(n, group, dq_ref, part_ref, dq_out, dk_out, dv_out):
    own_slot = ((lax.axis_index("ctx") + n - 2) % n) % group
    dq_out[...] = dq_ref[...]
    for kind, out in ((0, dk_out), (1, dv_out)):
        total = None
        for j, at, needed, slot in owner_turns(group, n > group, own_slot):
            part = part_ref[kind, at].astype(F32)
            total = part if total is None else total + jnp.where(needed, part, 0.0)
        out[...] = total.astype(BF16)


def local(queries, keys, values, out_grad, w_out, offsets):
    n = lax.axis_size("ctx")
    tok, width = queries.shape
    heads = offsets.shape[0]
    dim = width // heads
    feats = out_grad.shape[1]
    group = min(KEYS_SEG * 2 ** (LEVELS - 1), tok * n) // tok
    assert heads == 4 and tok * 4 == KEYS_SEG and lax.axis_size("tp") == 4
    assert n % group == 0 and group % 4 == 0
    pairs, rows, turns = group // 2, 2 * tok, group // 4
    wide = n > group
    slots = group + 2 * wide
    kinds = turns + wide
    dma = pltpu.SemaphoreType.DMA
    out = jax.ShapeDtypeStruct((tok, width), BF16)
    hbm = pl.BlockSpec(memory_space=pl.ANY)
    dq_raw, parts = pl.pallas_call(
        functools.partial(kernel, n),
        out_shape=(out, jax.ShapeDtypeStruct((2, kinds, tok, width), BF16)),
        in_specs=[hbm] * 5 + [pl.BlockSpec(memory_space=pltpu.SMEM)],
        out_specs=(hbm, hbm),
        scratch_shapes=[
            pltpu.VMEM(w_out.shape, BF16),
            pltpu.VMEM((4, tok, feats), BF16),
            pltpu.VMEM((tok, width), BF16),
            pltpu.VMEM((4 * tok, dim), BF16),
            pltpu.VMEM((4 * tok, dim), BF16),
            pltpu.VMEM((2, slots * tok, dim), BF16),
            pltpu.VMEM((2, pairs, rows, rows), F32),
            pltpu.VMEM((pairs, rows, rows), F32),
            pltpu.VMEM((rows, rows), BF16),
            pltpu.VMEM((rows, rows), BF16),
            pltpu.VMEM((2, slots * tok, dim), F32),
            pltpu.VMEM((2, slots * tok, dim), BF16),
            pltpu.VMEM((4 * tok, dim), BF16),
            dma, dma, dma((CHUNKS,)), dma((CHUNKS,)), dma((CHUNKS,)), dma((CHUNKS,)), dma, dma,
            dma((2, kinds, 4)), dma((2, slots)), dma((4,)), dma((4,)), dma((4,)), dma((4,)),
            dma((4,)), dma((4,)), dma((2, slots)), dma((2, kinds, 4)),
        ],
        compiler_params=pltpu.CompilerParams(
            collective_id=0, has_side_effects=True, vmem_limit_bytes=56 * 1024 * 1024
        ),
        cost_estimate=pl.CostEstimate(
            flops=5 * 10 * rows * rows * dim + 2 * tok * width * feats * 4,
            bytes_accessed=2 * (w_out.size + 8 * tok * width), transcendentals=5 * rows * rows,
        ),
    )(queries, keys, values, out_grad, w_out, offsets)
    steps = 2
    flat = pl.BlockSpec((tok // steps, width), lambda i: (i, 0))
    return pl.pallas_call(
        functools.partial(add_kernel, n, group),
        grid=(steps,),
        out_shape=(out, out, out),
        in_specs=[flat, pl.BlockSpec((2, kinds, tok // steps, width), lambda i: (0, 0, i, 0))],
        out_specs=(flat, flat, flat),
        compiler_params=pltpu.CompilerParams(vmem_limit_bytes=16 * 1024 * 1024),
    )(dq_raw, parts)


def solution(mesh):
    return jax.shard_map(
        local,
        mesh=mesh,
        in_specs=(
            P("ctx", "tp"),
            P("ctx", "tp"),
            P("ctx", "tp"),
            P("ctx", "tp"),
            P("tp", None),
            P("tp", None),
        ),
        out_specs=(P("ctx", "tp"), P("ctx", "tp"), P("ctx", "tp")),
        check_vma=False,
    )
```

```python
import functools
import math

import jax
import jax.numpy as jnp
from jax import lax
from jax.experimental import pallas as pl
from jax.experimental.pallas import tpu as pltpu
from jax.sharding import PartitionSpec as P

LEVELS = 3
KEYS_SEG = 1024
MESH = pl.DeviceIdType.MESH
NEGATIVE_FILL = -1e30
CHUNKS = 4
SUB = 128
F32 = jnp.float32
BF16 = jnp.bfloat16


def nt(a, b):
    return lax.dot_general(a, b, (((1,), (1,)), ((), ())), preferred_element_type=F32)


def tn(a, b):
    return lax.dot_general(a, b, (((0,), (0,)), ((), ())), preferred_element_type=F32)


def owner_turns(group, wide, own_slot):
    turns = group // 4
    listed = [(turns, turns - 1, own_slot < group, own_slot)]
    for j in range(1, turns):
        listed.append((j, j - 1, own_slot <= 4 * j + 1, own_slot))
    if wide:
        listed.append((0, turns, own_slot < 2, group + own_slot))
    return listed


def kernel(
    n, q_ref, k_ref, v_ref, og_ref, w_hbm, off_ref, dq_ref, part_buf,
    w_buf, og_buf, grad_buf, q_buf, g_buf, kv_buf, s_buf, p_buf, ds_buf, wl_buf,
    dkv_acc, dkv_low, dq_low,
    w_sem, og_sem, og_send, og_recv, fw_send, fw_recv, pair_send, pair_recv,
    kv_send, kv_recv, q_send, q_recv, g_send, g_recv,
    dq_send, dq_recv, part_send, part_recv,
):
    tok, width = q_ref.shape
    heads = off_ref.shape[0]
    dim = width // heads
    feats = og_ref.shape[1]
    group = min(KEYS_SEG * 2 ** (LEVELS - 1), tok * n) // tok
    pairs = group // 2
    rows = 2 * tok
    quads = n // 4
    turns = group // 4
    wide = n > group
    me = lax.axis_index("ctx")
    tp = lax.axis_index("tp")
    quad, head = me // 4, me % 4
    start = (4 * quad) % group
    straddle = start == 0
    u_block = (me + n - 2) % n
    own_group, own_slot = u_block // group, u_block % group
    first_group = ((4 * quad + n - 2) % n) // group
    core_peer = tp + 1 - 2 * (tp % 2)
    y_peer = (tp + 2) % 4
    far_peer = (core_peer + 2) % 4

    def move(src, dst, send, recv, target):
        @pl.when(target != me)
        def _():
            pltpu.make_async_remote_copy(
                src_ref=src, dst_ref=dst, send_sem=send, recv_sem=recv,
                device_id={"ctx": target}, device_id_type=MESH,
            ).start()

        @pl.when(target == me)
        def _():
            pltpu.make_async_copy(src, dst, recv).start()

    def sent(src, send, target):
        @pl.when(target != me)
        def _():
            pltpu.make_async_copy(src, src, send).wait()

    def arrived(dst, recv):
        pltpu.make_async_copy(dst, dst, recv).wait()

    def cols(index):
        return pl.ds(pl.multiple_of(index * dim, dim), dim)

    def block(index, size):
        return pl.ds(pl.multiple_of(index * size, size), size)

    w_copy = pltpu.make_async_copy(w_hbm, w_buf, w_sem)
    w_copy.start()
    og_copy = pltpu.make_async_copy(og_ref, og_buf.at[3], og_sem)
    og_copy.start()

    barrier = pltpu.get_barrier_semaphore()
    for step in range(1, n):
        pl.semaphore_signal(
            barrier, inc=1, device_id={"ctx": (me + step) % n}, device_id_type=MESH
        )
    for peer in (core_peer, y_peer):
        pl.semaphore_signal(barrier, inc=1, device_id={"tp": peer}, device_id_type=MESH)
    pl.semaphore_wait(barrier, n + 1)

    def tp_copy(src, dst, send, recv, peer):
        return pltpu.make_async_remote_copy(
            src_ref=src, dst_ref=dst, send_sem=send, recv_sem=recv,
            device_id={"tp": peer}, device_id_type=MESH,
        )

    piece = feats // CHUNKS
    for c in range(CHUNKS):
        part = pl.ds(c * piece, piece)
        tp_copy(
            og_ref.at[:, part], og_buf.at[1, :, part], og_send.at[c], og_recv.at[c], y_peer
        ).start()
    tp_copy(og_ref, og_buf.at[0], pair_send, pair_recv, core_peer).start()

    sources = (k_ref, v_ref)
    turn_list = owner_turns(group, wide, own_slot)

    def send_kv(act, kind, entry):
        j, at, needed, slot = entry

        @pl.when(needed)
        def _():
            to_quad = (own_group * turns + j) % quads
            for h in range(4):
                act(kind, at, h, slot, 4 * to_quad + h)

    def start_kv(kind, at, h, slot, target):
        move(
            sources[kind].at[:, pl.ds(h * dim, dim)], kv_buf.at[kind, block(slot, tok)],
            kv_send.at[kind, at, h], kv_recv.at[kind, slot], target,
        )

    send_kv(start_kv, 0, turn_list[0])
    for h in range(4):
        move(
            q_ref.at[:, pl.ds(h * dim, dim)], q_buf.at[block(head, tok)],
            q_send.at[h], q_recv.at[head], 4 * quad + h,
        )
    send_kv(start_kv, 1, turn_list[0])
    for kind in range(2):
        for entry in turn_list[1:]:
            send_kv(start_kv, kind, entry)

    dkv_acc[...] = jnp.zeros_like(dkv_acc)

    w_copy.wait()
    og_copy.wait()

    def w_part(shard, c):
        return w_buf[:, pl.ds(pl.multiple_of(shard * feats + c * piece, piece), piece)]

    total = nt(og_buf[3], w_buf[:, block(tp, feats)])
    arrived(og_buf.at[0], pair_recv)
    total += nt(og_buf[0], w_buf[:, block(core_peer, feats)])
    for c in range(CHUNKS):
        part = pl.ds(c * piece, piece)
        arrived(og_buf.at[1, :, part], og_recv.at[c])
        tp_copy(
            og_buf.at[1, :, part], og_buf.at[2, :, part], fw_send.at[c], fw_recv.at[c], core_peer
        ).start()
        total += nt(og_buf[1, :, part], w_part(y_peer, c))
    for c in range(CHUNKS):
        part = pl.ds(c * piece, piece)
        arrived(og_buf.at[2, :, part], fw_recv.at[c])
        total += nt(og_buf[2, :, part], w_part(far_peer, c))
    grad_buf[...] = total.astype(BF16)
    for h in range(4):
        move(
            grad_buf.at[:, pl.ds(h * dim, dim)], g_buf.at[block(head, tok)],
            g_send.at[h], g_recv.at[head], 4 * quad + h,
        )

    def wait_pair(kind, pair):
        for b in range(2):
            slot = 2 * pair + b
            arrived(kv_buf.at[kind, block(slot, tok)], kv_recv.at[kind, slot])

    for b in range(4):
        arrived(q_buf.at[block(b, tok)], q_recv.at[b])

    odd1, odd2 = off_ref[head, 1], off_ref[head, 2]
    key_row = lax.broadcasted_iota(jnp.int32, (8, rows), 0)
    query_col = lax.broadcasted_iota(jnp.int32, (8, rows), 1)
    both1 = ((key_row % 2 == odd1) & (query_col % 2 == odd1)).astype(F32)
    both2 = ((key_row % 4 == odd2) & (query_col % 4 == odd2)).astype(F32)
    sub_row = lax.broadcasted_iota(jnp.int32, (SUB, rows), 0)
    sub_col = lax.broadcasted_iota(jnp.int32, (SUB, rows), 1)
    score_scale = 1.0 / math.sqrt(dim)
    to_exp2 = score_scale / math.log(2.0)
    first_pair = jnp.where(straddle, 0, start // 2 - 1)
    first_base = jnp.where(straddle, pairs, 0) if wide else 0
    last_pair = jnp.where(straddle, pairs - 1, start // 2)
    early = jnp.where(straddle, 1, 0)
    halves = [(early, first_pair, first_base), (1 - early, last_pair, 0)]

    def arrival(turn, step):
        count = halves[turn][1] + 1
        return step if turn == 0 else (step + jnp.where(straddle, count - 1, 1)) % count

    def wait_new(turn, kind, kp):
        if turn == 0:
            wait_pair(kind, first_base + kp)
        else:
            fresh = kp > first_pair
            if wide:
                fresh = fresh | straddle
            pl.when(fresh)(functools.partial(wait_pair, kind, kp))

    def folded(values):
        return values.reshape(values.shape[0] // 8, 8, values.shape[1])

    tops = []
    for turn, (half, at_pair, base) in enumerate(halves):
        queries = q_buf[block(half, rows), :]

        def score_body(step, top, turn=turn, at_pair=at_pair, base=base, queries=queries):
            kp = arrival(turn, step)
            wait_new(turn, 0, kp)
            same0 = jnp.where(at_pair // 2 == kp // 2, 1.0, 0.0)
            same1 = jnp.where(at_pair // 4 == kp // 4, 1.0, 0.0)
            count = same0 + same1 * both1 + both2
            bias = jnp.where(
                count > 2.5, math.log2(3.0),
                jnp.where(count > 1.5, 1.0, jnp.where(count > 0.5, 0.0, NEGATIVE_FILL)),
            )
            lead = (at_pair - kp) * rows
            for s in range(rows // SUB):
                keys = kv_buf[0, pl.ds(pl.multiple_of((base + kp) * rows + s * SUB, SUB), SUB), :]
                scores = folded(nt(keys, queries) * to_exp2) + bias[None]
                scores = scores.reshape(SUB, rows)
                scores = jnp.where(sub_row + s * SUB <= sub_col + lead, scores, NEGATIVE_FILL)
                s_buf[turn, kp, s * SUB:(s + 1) * SUB, :] = scores
                top = jnp.maximum(top, jnp.max(folded(scores), axis=0))
            return top

        top = lax.fori_loop(
            0, at_pair + 1, score_body, jnp.full((8, rows), NEGATIVE_FILL, F32)
        )
        tops.append(jnp.max(top, axis=0, keepdims=True))

    part_at = jnp.where(straddle, turns, start // 4) - 1

    def slot_owner(slot):
        return (first_group * group + slot + 2) % n

    def send_slot(kind, slot, owner, at):
        move(
            dkv_low.at[kind, block(slot, tok)], part_buf.at[kind, at, :, cols(head)],
            part_send.at[kind, slot], part_recv.at[kind, at, head], owner,
        )

    def round_pair(kind, kp):
        done = dkv_acc[kind, block(kp, rows), :]
        if kind == 0:
            done = done * score_scale
        dkv_low[kind, block(kp, rows), :] = done.astype(BF16)

    def send_pair(kind, kp):
        round_pair(kind, kp)
        for b in range(2):
            slot = 2 * kp + b
            send_slot(kind, slot, slot_owner(slot), part_at)

    def leaving(turn, step):
        if turn == 0:
            return step
        return (step + jnp.where(straddle, 1, 0)) % (halves[1][1] + 1)

    zero = jnp.zeros((8, rows), F32)
    inverses = []
    for turn, (half, at_pair, base) in enumerate(halves):
        def weigh_body(step, den, turn=turn, top=tops[turn]):
            for s in range(rows // SUB):
                here = slice(s * SUB, (s + 1) * SUB)
                weight = jnp.exp2(s_buf[turn, step, here, :] - top)
                s_buf[turn, step, here, :] = weight
                den = den + jnp.sum(folded(weight), axis=0)
            return den

        den = lax.fori_loop(0, at_pair + 1, weigh_body, zero)
        inverses.append(1.0 / jnp.sum(den, axis=0, keepdims=True))

    for turn, (half, at_pair, base) in enumerate(halves):
        for b in range(2):
            arrived(g_buf.at[block(2 * half + b, tok)], g_recv.at[2 * half + b])
        grads = g_buf[block(half, rows), :]

        def value_body(step, none, turn=turn, base=base, grads=grads):
            kp = leaving(turn, step)
            for s in range(rows // SUB):
                here = slice(s * SUB, (s + 1) * SUB)
                weight = s_buf[turn, kp, here, :] * inverses[turn]
                s_buf[turn, kp, here, :] = weight
                wl_buf[here, :] = weight.astype(BF16)
            place = block(base + kp, rows)
            dkv_acc[1, place, :] += jnp.dot(wl_buf[...], grads, preferred_element_type=F32)
            if turn == 1:
                send_pair(1, kp)
            return none

        lax.fori_loop(0, at_pair + 1, value_body, 0)

    for turn, (half, at_pair, base) in enumerate(halves):
        queries = q_buf[block(half, rows), :]
        grads = g_buf[block(half, rows), :]

        def prob_body(step, num, turn=turn, base=base, grads=grads):
            kp = arrival(turn, step)
            wait_new(turn, 1, kp)
            for s in range(rows // SUB):
                here = slice(s * SUB, (s + 1) * SUB)
                vals = kv_buf[1, pl.ds(pl.multiple_of((base + kp) * rows + s * SUB, SUB), SUB), :]
                prob = nt(vals, grads)
                p_buf[kp, here, :] = prob
                num = num + jnp.sum(folded(s_buf[turn, kp, here, :] * prob), axis=0)
            return num

        num = lax.fori_loop(0, at_pair + 1, prob_body, zero)
        delta = jnp.sum(num, axis=0, keepdims=True)

        def grad_body(step, total, turn=turn, base=base, queries=queries, delta=delta):
            kp = leaving(turn, step)
            for s in range(rows // SUB):
                here = slice(s * SUB, (s + 1) * SUB)
                ds_buf[here, :] = (
                    s_buf[turn, kp, here, :] * (p_buf[kp, here, :] - delta)
                ).astype(BF16)
            place = block(base + kp, rows)
            score_grad = ds_buf[...]
            dkv_acc[0, place, :] += jnp.dot(score_grad, queries, preferred_element_type=F32)
            if turn == 1:
                send_pair(0, kp)
            return total + tn(kv_buf[0, place, :], score_grad)

        total = lax.fori_loop(0, at_pair + 1, grad_body, jnp.zeros((dim, rows), F32))
        dq_low[block(half, rows), :] = (total * score_scale).T.astype(BF16)
        for b in range(2):
            move(
                dq_low.at[block(2 * half + b, tok)], dq_ref.at[:, cols(head)],
                dq_send.at[2 * half + b], dq_recv.at[head], 4 * quad + 2 * half + b,
            )
    if wide:
        @pl.when(straddle)
        def _():
            for kind in range(2):
                round_pair(kind, pairs)
                for b in range(2):
                    send_slot(kind, group + b, (4 * quad + b + 2) % n, turns)

    for j, at, needed, slot in turn_list:
        @pl.when(needed)
        def _(at=at):
            for kind in range(2):
                for h in range(4):
                    arrived(part_buf.at[kind, at, :, pl.ds(h * dim, dim)], part_recv.at[kind, at, h])
    for h in range(4):
        arrived(dq_ref.at[:, pl.ds(h * dim, dim)], dq_recv.at[h])

    for c in range(CHUNKS):
        part = pl.ds(c * piece, piece)
        pltpu.make_async_copy(og_ref.at[:, part], og_ref.at[:, part], og_send.at[c]).wait()
        pltpu.make_async_copy(og_ref.at[:, part], og_ref.at[:, part], fw_send.at[c]).wait()
    pltpu.make_async_copy(og_ref, og_ref, pair_send).wait()
    for h in range(4):
        sent(q_ref.at[:, pl.ds(h * dim, dim)], q_send.at[h], 4 * quad + h)
        sent(grad_buf.at[:, pl.ds(h * dim, dim)], g_send.at[h], 4 * quad + h)
        sent(dq_low.at[pl.ds(h * tok, tok)], dq_send.at[h], 4 * quad + h)

    def kv_sent(kind, at, h, slot, target):
        sent(sources[kind].at[:, pl.ds(h * dim, dim)], kv_send.at[kind, at, h], target)

    for kind in range(2):
        for entry in turn_list:
            send_kv(kv_sent, kind, entry)

    def slot_sent(slot):
        owner = slot_owner(slot) if slot < group else (4 * quad + slot - group + 2) % n
        for kind in range(2):
            sent(dkv_low.at[kind, pl.ds(slot * tok, tok)], part_send.at[kind, slot], owner)

    for slot in range(group + 2 * wide):
        needed = straddle | (slot <= start + 1) if slot < group else straddle
        pl.when(needed)(functools.partial(slot_sent, slot))


def add_kernel(n, group, dq_ref, part_ref, dq_out, dk_out, dv_out):
    own_slot = ((lax.axis_index("ctx") + n - 2) % n) % group
    dq_out[...] = dq_ref[...]
    for kind, out in ((0, dk_out), (1, dv_out)):
        total = None
        for j, at, needed, slot in owner_turns(group, n > group, own_slot):
            part = part_ref[kind, at].astype(F32)
            total = part if total is None else total + jnp.where(needed, part, 0.0)
        out[...] = total.astype(BF16)


def local(queries, keys, values, out_grad, w_out, offsets):
    n = lax.axis_size("ctx")
    tok, width = queries.shape
    heads = offsets.shape[0]
    dim = width // heads
    feats = out_grad.shape[1]
    group = min(KEYS_SEG * 2 ** (LEVELS - 1), tok * n) // tok
    assert heads == 4 and tok * 4 == KEYS_SEG and lax.axis_size("tp") == 4
    assert n % group == 0 and group % 4 == 0
    pairs, rows, turns = group // 2, 2 * tok, group // 4
    wide = n > group
    slots = group + 2 * wide
    kinds = turns + wide
    dma = pltpu.SemaphoreType.DMA
    out = jax.ShapeDtypeStruct((tok, width), BF16)
    hbm = pl.BlockSpec(memory_space=pl.ANY)
    dq_raw, parts = pl.pallas_call(
        functools.partial(kernel, n),
        out_shape=(out, jax.ShapeDtypeStruct((2, kinds, tok, width), BF16)),
        in_specs=[hbm] * 5 + [pl.BlockSpec(memory_space=pltpu.SMEM)],
        out_specs=(hbm, hbm),
        scratch_shapes=[
            pltpu.VMEM(w_out.shape, BF16),
            pltpu.VMEM((4, tok, feats), BF16),
            pltpu.VMEM((tok, width), BF16),
            pltpu.VMEM((4 * tok, dim), BF16),
            pltpu.VMEM((4 * tok, dim), BF16),
            pltpu.VMEM((2, slots * tok, dim), BF16),
            pltpu.VMEM((2, pairs, rows, rows), F32),
            pltpu.VMEM((pairs, rows, rows), F32),
            pltpu.VMEM((rows, rows), BF16),
            pltpu.VMEM((rows, rows), BF16),
            pltpu.VMEM((2, slots * tok, dim), F32),
            pltpu.VMEM((2, slots * tok, dim), BF16),
            pltpu.VMEM((4 * tok, dim), BF16),
            dma, dma, dma((CHUNKS,)), dma((CHUNKS,)), dma((CHUNKS,)), dma((CHUNKS,)), dma, dma,
            dma((2, kinds, 4)), dma((2, slots)), dma((4,)), dma((4,)), dma((4,)), dma((4,)),
            dma((4,)), dma((4,)), dma((2, slots)), dma((2, kinds, 4)),
        ],
        compiler_params=pltpu.CompilerParams(
            collective_id=0, has_side_effects=True, vmem_limit_bytes=56 * 1024 * 1024
        ),
        cost_estimate=pl.CostEstimate(
            flops=5 * 10 * rows * rows * dim + 2 * tok * width * feats * 4,
            bytes_accessed=2 * (w_out.size + 8 * tok * width), transcendentals=5 * rows * rows,
        ),
    )(queries, keys, values, out_grad, w_out, offsets)
    steps = 2
    flat = pl.BlockSpec((tok // steps, width), lambda i: (i, 0))
    return pl.pallas_call(
        functools.partial(add_kernel, n, group),
        grid=(steps,),
        out_shape=(out, out, out),
        in_specs=[flat, pl.BlockSpec((2, kinds, tok // steps, width), lambda i: (0, 0, i, 0))],
        out_specs=(flat, flat, flat),
        compiler_params=pltpu.CompilerParams(vmem_limit_bytes=60 * 1024 * 1024),
    )(dq_raw, parts)


def solution(mesh):
    return jax.shard_map(
        local,
        mesh=mesh,
        in_specs=(
            P("ctx", "tp"),
            P("ctx", "tp"),
            P("ctx", "tp"),
            P("ctx", "tp"),
            P("tp", None),
            P("tp", None),
        ),
        out_specs=(P("ctx", "tp"), P("ctx", "tp"), P("ctx", "tp")),
        check_vma=False,
    )
```

```python
import functools
import math

import jax
import jax.numpy as jnp
from jax import lax
from jax.experimental import pallas as pl
from jax.experimental.pallas import tpu as pltpu
from jax.sharding import PartitionSpec as P

LEVELS = 3
KEYS_SEG = 1024
MESH = pl.DeviceIdType.MESH
NEGATIVE_FILL = -1e30
CHUNKS = 4
SUB = 128
F32 = jnp.float32
BF16 = jnp.bfloat16


def nt(a, b):
    return lax.dot_general(a, b, (((1,), (1,)), ((), ())), preferred_element_type=F32)


def tn(a, b):
    return lax.dot_general(a, b, (((0,), (0,)), ((), ())), preferred_element_type=F32)


def owner_turns(group, wide, own_slot):
    turns = group // 4
    listed = [(turns, turns - 1, own_slot < group, own_slot)]
    for j in range(1, turns):
        listed.append((j, j - 1, own_slot <= 4 * j + 1, own_slot))
    if wide:
        listed.append((0, turns, own_slot < 2, group + own_slot))
    return listed


def kernel(
    n, q_ref, k_ref, v_ref, og_ref, w_hbm, off_ref, dq_ref, part_buf,
    w_buf, og_buf, stage, grad_buf, q_buf, g_buf, kv_buf, s_buf, p_buf, ds_buf, wl_buf,
    dkv_acc, dkv_low, dq_low,
    w_sem, og_sem, stage_sem, og_send, og_recv, fw_send, fw_recv, pair_send, pair_recv,
    kv_send, kv_recv, q_send, q_recv, g_send, g_recv,
    dq_send, dq_recv, part_send, part_recv,
):
    tok, width = q_ref.shape
    heads = off_ref.shape[0]
    dim = width // heads
    feats = og_ref.shape[1]
    group = min(KEYS_SEG * 2 ** (LEVELS - 1), tok * n) // tok
    pairs = group // 2
    rows = 2 * tok
    quads = n // 4
    turns = group // 4
    wide = n > group
    me = lax.axis_index("ctx")
    tp = lax.axis_index("tp")
    quad, head = me // 4, me % 4
    start = (4 * quad) % group
    straddle = start == 0
    u_block = (me + n - 2) % n
    own_group, own_slot = u_block // group, u_block % group
    first_group = ((4 * quad + n - 2) % n) // group
    core_peer = tp + 1 - 2 * (tp % 2)
    y_peer = (tp + 2) % 4
    far_peer = (core_peer + 2) % 4

    def move(src, dst, send, recv, target):
        @pl.when(target != me)
        def _():
            pltpu.make_async_remote_copy(
                src_ref=src, dst_ref=dst, send_sem=send, recv_sem=recv,
                device_id={"ctx": target}, device_id_type=MESH,
            ).start()

        @pl.when(target == me)
        def _():
            pltpu.make_async_copy(src, dst, recv).start()

    def sent(src, send, target):
        @pl.when(target != me)
        def _():
            pltpu.make_async_copy(src, src, send).wait()

    def arrived(dst, recv):
        pltpu.make_async_copy(dst, dst, recv).wait()

    def block(index, size):
        return pl.ds(pl.multiple_of(index * size, size), size)

    staged = []
    for kind, ref in enumerate((k_ref, v_ref, q_ref)):
        for h in range(4):
            staged.append(pltpu.make_async_copy(
                ref.at[:, pl.ds(h * dim, dim)], stage.at[kind, h], stage_sem.at[kind, h]
            ))
            staged[-1].start()
    w_copy = pltpu.make_async_copy(w_hbm, w_buf, w_sem)
    w_copy.start()
    og_copy = pltpu.make_async_copy(og_ref, og_buf.at[3], og_sem)
    og_copy.start()

    barrier = pltpu.get_barrier_semaphore()
    for step in range(1, n):
        pl.semaphore_signal(
            barrier, inc=1, device_id={"ctx": (me + step) % n}, device_id_type=MESH
        )
    for peer in (core_peer, y_peer):
        pl.semaphore_signal(barrier, inc=1, device_id={"tp": peer}, device_id_type=MESH)
    pl.semaphore_wait(barrier, n + 1)

    def tp_copy(src, dst, send, recv, peer):
        return pltpu.make_async_remote_copy(
            src_ref=src, dst_ref=dst, send_sem=send, recv_sem=recv,
            device_id={"tp": peer}, device_id_type=MESH,
        )

    piece = feats // CHUNKS
    for c in range(CHUNKS):
        part = pl.ds(c * piece, piece)
        tp_copy(
            og_ref.at[:, part], og_buf.at[1, :, part], og_send.at[c], og_recv.at[c], y_peer
        ).start()
    tp_copy(og_ref, og_buf.at[0], pair_send, pair_recv, core_peer).start()

    for copy in staged:
        copy.wait()
    turn_list = owner_turns(group, wide, own_slot)

    def send_kv(act, kind, entry):
        j, at, needed, slot = entry

        @pl.when(needed)
        def _():
            to_quad = (own_group * turns + j) % quads
            for h in range(4):
                act(kind, at, h, slot, 4 * to_quad + h)

    def start_kv(kind, at, h, slot, target):
        move(
            stage.at[kind, h], kv_buf.at[kind, block(slot, tok)],
            kv_send.at[kind, at, h], kv_recv.at[kind, slot], target,
        )

    send_kv(start_kv, 0, turn_list[0])
    for h in range(4):
        move(
            stage.at[2, h], q_buf.at[block(head, tok)],
            q_send.at[h], q_recv.at[head], 4 * quad + h,
        )
    for entry in turn_list[1:]:
        send_kv(start_kv, 0, entry)

    dkv_acc[...] = jnp.zeros_like(dkv_acc)

    w_copy.wait()
    og_copy.wait()

    def w_part(shard, c):
        return w_buf[:, pl.ds(pl.multiple_of(shard * feats + c * piece, piece), piece)]

    total = nt(og_buf[3], w_buf[:, block(tp, feats)])
    arrived(og_buf.at[0], pair_recv)
    total += nt(og_buf[0], w_buf[:, block(core_peer, feats)])
    for c in range(CHUNKS):
        part = pl.ds(c * piece, piece)
        arrived(og_buf.at[1, :, part], og_recv.at[c])
        tp_copy(
            og_buf.at[1, :, part], og_buf.at[2, :, part], fw_send.at[c], fw_recv.at[c], core_peer
        ).start()
        total += nt(og_buf[1, :, part], w_part(y_peer, c))
    for c in range(CHUNKS):
        part = pl.ds(c * piece, piece)
        arrived(og_buf.at[2, :, part], fw_recv.at[c])
        total += nt(og_buf[2, :, part], w_part(far_peer, c))
    for h in range(4):
        grad_buf[h] = total[:, h * dim:(h + 1) * dim].astype(BF16)
        move(
            grad_buf.at[h], g_buf.at[block(head, tok)],
            g_send.at[h], g_recv.at[head], 4 * quad + h,
        )

    for entry in turn_list:
        send_kv(start_kv, 1, entry)

    def wait_pair(kind, pair):
        for b in range(2):
            slot = 2 * pair + b
            arrived(kv_buf.at[kind, block(slot, tok)], kv_recv.at[kind, slot])

    for b in range(4):
        arrived(q_buf.at[block(b, tok)], q_recv.at[b])

    odd1, odd2 = off_ref[head, 1], off_ref[head, 2]
    key_row = lax.broadcasted_iota(jnp.int32, (8, rows), 0)
    query_col = lax.broadcasted_iota(jnp.int32, (8, rows), 1)
    both1 = ((key_row % 2 == odd1) & (query_col % 2 == odd1)).astype(F32)
    both2 = ((key_row % 4 == odd2) & (query_col % 4 == odd2)).astype(F32)
    sub_row = lax.broadcasted_iota(jnp.int32, (SUB, rows), 0)
    sub_col = lax.broadcasted_iota(jnp.int32, (SUB, rows), 1)
    score_scale = 1.0 / math.sqrt(dim)
    to_exp2 = score_scale / math.log(2.0)
    first_pair = jnp.where(straddle, 0, start // 2 - 1)
    first_base = jnp.where(straddle, pairs, 0) if wide else 0
    last_pair = jnp.where(straddle, pairs - 1, start // 2)
    early = jnp.where(straddle, 1, 0)
    halves = [(early, first_pair, first_base), (1 - early, last_pair, 0)]

    def arrival(turn, step):
        count = halves[turn][1] + 1
        return step if turn == 0 else (step + jnp.where(straddle, count - 1, 1)) % count

    def wait_new(turn, kind, kp):
        if turn == 0:
            wait_pair(kind, first_base + kp)
        else:
            fresh = kp > first_pair
            if wide:
                fresh = fresh | straddle
            pl.when(fresh)(functools.partial(wait_pair, kind, kp))

    def folded(values):
        return values.reshape(values.shape[0] // 8, 8, values.shape[1])

    tops = []
    for turn, (half, at_pair, base) in enumerate(halves):
        queries = q_buf[block(half, rows), :]

        def score_body(step, top, turn=turn, at_pair=at_pair, base=base, queries=queries):
            kp = arrival(turn, step)
            wait_new(turn, 0, kp)
            same0 = jnp.where(at_pair // 2 == kp // 2, 1.0, 0.0)
            same1 = jnp.where(at_pair // 4 == kp // 4, 1.0, 0.0)
            count = same0 + same1 * both1 + both2
            bias = jnp.where(
                count > 2.5, math.log2(3.0),
                jnp.where(count > 1.5, 1.0, jnp.where(count > 0.5, 0.0, NEGATIVE_FILL)),
            )
            lead = (at_pair - kp) * rows
            for s in range(rows // SUB):
                keys = kv_buf[0, pl.ds(pl.multiple_of((base + kp) * rows + s * SUB, SUB), SUB), :]
                scores = folded(nt(keys, queries) * to_exp2) + bias[None]
                scores = scores.reshape(SUB, rows)
                scores = jnp.where(sub_row + s * SUB <= sub_col + lead, scores, NEGATIVE_FILL)
                s_buf[turn, kp, s * SUB:(s + 1) * SUB, :] = scores
                top = jnp.maximum(top, jnp.max(folded(scores), axis=0))
            return top

        top = lax.fori_loop(
            0, at_pair + 1, score_body, jnp.full((8, rows), NEGATIVE_FILL, F32)
        )
        tops.append(jnp.max(top, axis=0, keepdims=True))

    part_at = jnp.where(straddle, turns, start // 4) - 1

    def slot_owner(slot):
        return (first_group * group + slot + 2) % n

    def send_slot(kind, slot, owner, at):
        move(
            dkv_low.at[kind, block(slot, tok)], part_buf.at[kind, at, head],
            part_send.at[kind, slot], part_recv.at[kind, at, head], owner,
        )

    def round_pair(kind, kp):
        done = dkv_acc[kind, block(kp, rows), :]
        if kind == 0:
            done = done * score_scale
        dkv_low[kind, block(kp, rows), :] = done.astype(BF16)

    def send_pair(kind, kp):
        round_pair(kind, kp)
        for b in range(2):
            slot = 2 * kp + b
            send_slot(kind, slot, slot_owner(slot), part_at)

    def leaving(turn, step):
        if turn == 0:
            return step
        return (step + jnp.where(straddle, 1, 0)) % (halves[1][1] + 1)

    zero = jnp.zeros((8, rows), F32)
    inverses = []
    for turn, (half, at_pair, base) in enumerate(halves):
        def weigh_body(step, den, turn=turn, top=tops[turn]):
            for s in range(rows // SUB):
                here = slice(s * SUB, (s + 1) * SUB)
                weight = jnp.exp2(s_buf[turn, step, here, :] - top)
                s_buf[turn, step, here, :] = weight
                den = den + jnp.sum(folded(weight), axis=0)
            return den

        den = lax.fori_loop(0, at_pair + 1, weigh_body, zero)
        inverses.append(1.0 / jnp.sum(den, axis=0, keepdims=True))

    for turn, (half, at_pair, base) in enumerate(halves):
        for b in range(2):
            arrived(g_buf.at[block(2 * half + b, tok)], g_recv.at[2 * half + b])
        grads = g_buf[block(half, rows), :]

        def value_body(step, none, turn=turn, base=base, grads=grads):
            kp = leaving(turn, step)
            for s in range(rows // SUB):
                here = slice(s * SUB, (s + 1) * SUB)
                weight = s_buf[turn, kp, here, :] * inverses[turn]
                s_buf[turn, kp, here, :] = weight
                wl_buf[here, :] = weight.astype(BF16)
            place = block(base + kp, rows)
            dkv_acc[1, place, :] += jnp.dot(wl_buf[...], grads, preferred_element_type=F32)
            if turn == 1:
                send_pair(1, kp)
            return none

        lax.fori_loop(0, at_pair + 1, value_body, 0)

    for turn, (half, at_pair, base) in enumerate(halves):
        queries = q_buf[block(half, rows), :]
        grads = g_buf[block(half, rows), :]

        def prob_body(step, num, turn=turn, base=base, grads=grads):
            kp = arrival(turn, step)
            wait_new(turn, 1, kp)
            for s in range(rows // SUB):
                here = slice(s * SUB, (s + 1) * SUB)
                vals = kv_buf[1, pl.ds(pl.multiple_of((base + kp) * rows + s * SUB, SUB), SUB), :]
                prob = nt(vals, grads)
                p_buf[kp, here, :] = prob
                num = num + jnp.sum(folded(s_buf[turn, kp, here, :] * prob), axis=0)
            return num

        num = lax.fori_loop(0, at_pair + 1, prob_body, zero)
        delta = jnp.sum(num, axis=0, keepdims=True)

        def grad_body(step, total, turn=turn, base=base, queries=queries, delta=delta):
            kp = leaving(turn, step)
            for s in range(rows // SUB):
                here = slice(s * SUB, (s + 1) * SUB)
                ds_buf[here, :] = (
                    s_buf[turn, kp, here, :] * (p_buf[kp, here, :] - delta)
                ).astype(BF16)
            place = block(base + kp, rows)
            score_grad = ds_buf[...]
            dkv_acc[0, place, :] += jnp.dot(score_grad, queries, preferred_element_type=F32)
            if turn == 1:
                send_pair(0, kp)
            return total + tn(kv_buf[0, place, :], score_grad)

        total = lax.fori_loop(0, at_pair + 1, grad_body, jnp.zeros((dim, rows), F32))
        dq_low[block(half, rows), :] = (total * score_scale).T.astype(BF16)
        for b in range(2):
            move(
                dq_low.at[block(2 * half + b, tok)], dq_ref.at[head],
                dq_send.at[2 * half + b], dq_recv.at[head], 4 * quad + 2 * half + b,
            )
    if wide:
        @pl.when(straddle)
        def _():
            for kind in range(2):
                round_pair(kind, pairs)
                for b in range(2):
                    send_slot(kind, group + b, (4 * quad + b + 2) % n, turns)

    for j, at, needed, slot in turn_list:
        @pl.when(needed)
        def _(at=at):
            for kind in range(2):
                for h in range(4):
                    arrived(part_buf.at[kind, at, h], part_recv.at[kind, at, h])
    for h in range(4):
        arrived(dq_ref.at[h], dq_recv.at[h])

    for c in range(CHUNKS):
        part = pl.ds(c * piece, piece)
        pltpu.make_async_copy(og_ref.at[:, part], og_ref.at[:, part], og_send.at[c]).wait()
        pltpu.make_async_copy(og_ref.at[:, part], og_ref.at[:, part], fw_send.at[c]).wait()
    pltpu.make_async_copy(og_ref, og_ref, pair_send).wait()
    for h in range(4):
        sent(stage.at[2, h], q_send.at[h], 4 * quad + h)
        sent(grad_buf.at[h], g_send.at[h], 4 * quad + h)
        sent(dq_low.at[pl.ds(h * tok, tok)], dq_send.at[h], 4 * quad + h)

    def kv_sent(kind, at, h, slot, target):
        sent(stage.at[kind, h], kv_send.at[kind, at, h], target)

    for kind in range(2):
        for entry in turn_list:
            send_kv(kv_sent, kind, entry)

    def slot_sent(slot):
        owner = slot_owner(slot) if slot < group else (4 * quad + slot - group + 2) % n
        for kind in range(2):
            sent(dkv_low.at[kind, pl.ds(slot * tok, tok)], part_send.at[kind, slot], owner)

    for slot in range(group + 2 * wide):
        needed = straddle | (slot <= start + 1) if slot < group else straddle
        pl.when(needed)(functools.partial(slot_sent, slot))


def add_kernel(n, group, dq_ref, part_ref, dq_out, dk_out, dv_out):
    own_slot = ((lax.axis_index("ctx") + n - 2) % n) % group
    dim = dq_ref.shape[2]
    for h in range(4):
        here = slice(h * dim, (h + 1) * dim)
        dq_out[:, here] = dq_ref[h]
        for kind, out in ((0, dk_out), (1, dv_out)):
            total = None
            for j, at, needed, slot in owner_turns(group, n > group, own_slot):
                part = part_ref[kind, at, h].astype(F32)
                total = part if total is None else total + jnp.where(needed, part, 0.0)
            out[:, here] = total.astype(BF16)


def local(queries, keys, values, out_grad, w_out, offsets):
    n = lax.axis_size("ctx")
    tok, width = queries.shape
    heads = offsets.shape[0]
    dim = width // heads
    feats = out_grad.shape[1]
    group = min(KEYS_SEG * 2 ** (LEVELS - 1), tok * n) // tok
    assert heads == 4 and tok * 4 == KEYS_SEG and lax.axis_size("tp") == 4
    assert n % group == 0 and group % 4 == 0
    pairs, rows, turns = group // 2, 2 * tok, group // 4
    wide = n > group
    slots = group + 2 * wide
    kinds = turns + wide
    dma = pltpu.SemaphoreType.DMA
    out = jax.ShapeDtypeStruct((tok, width), BF16)
    hbm = pl.BlockSpec(memory_space=pl.ANY)
    dq_raw, parts = pl.pallas_call(
        functools.partial(kernel, n),
        out_shape=(
            jax.ShapeDtypeStruct((4, tok, dim), BF16),
            jax.ShapeDtypeStruct((2, kinds, 4, tok, dim), BF16),
        ),
        in_specs=[hbm] * 5 + [pl.BlockSpec(memory_space=pltpu.SMEM)],
        out_specs=(hbm, hbm),
        scratch_shapes=[
            pltpu.VMEM(w_out.shape, BF16),
            pltpu.VMEM((4, tok, feats), BF16),
            pltpu.VMEM((3, 4, tok, dim), BF16),
            pltpu.VMEM((4, tok, dim), BF16),
            pltpu.VMEM((4 * tok, dim), BF16),
            pltpu.VMEM((4 * tok, dim), BF16),
            pltpu.VMEM((2, slots * tok, dim), BF16),
            pltpu.VMEM((2, pairs, rows, rows), F32),
            pltpu.VMEM((pairs, rows, rows), F32),
            pltpu.VMEM((rows, rows), BF16),
            pltpu.VMEM((rows, rows), BF16),
            pltpu.VMEM((2, slots * tok, dim), F32),
            pltpu.VMEM((2, slots * tok, dim), BF16),
            pltpu.VMEM((4 * tok, dim), BF16),
            dma, dma, dma((3, 4)), dma((CHUNKS,)), dma((CHUNKS,)), dma((CHUNKS,)), dma((CHUNKS,)), dma, dma,
            dma((2, kinds, 4)), dma((2, slots)), dma((4,)), dma((4,)), dma((4,)), dma((4,)),
            dma((4,)), dma((4,)), dma((2, slots)), dma((2, kinds, 4)),
        ],
        compiler_params=pltpu.CompilerParams(
            collective_id=0, has_side_effects=True, vmem_limit_bytes=56 * 1024 * 1024
        ),
        cost_estimate=pl.CostEstimate(
            flops=5 * 10 * rows * rows * dim + 2 * tok * width * feats * 4,
            bytes_accessed=2 * (w_out.size + 8 * tok * width), transcendentals=5 * rows * rows,
        ),
    )(queries, keys, values, out_grad, w_out, offsets)
    steps = 2
    flat = pl.BlockSpec((tok // steps, width), lambda i: (i, 0))
    return pl.pallas_call(
        functools.partial(add_kernel, n, group),
        grid=(steps,),
        out_shape=(out, out, out),
        in_specs=[
            pl.BlockSpec((4, tok // steps, dim), lambda i: (0, i, 0)),
            pl.BlockSpec((2, kinds, 4, tok // steps, dim), lambda i: (0, 0, 0, i, 0)),
        ],
        out_specs=(flat, flat, flat),
        compiler_params=pltpu.CompilerParams(vmem_limit_bytes=60 * 1024 * 1024),
    )(dq_raw, parts)


def solution(mesh):
    return jax.shard_map(
        local,
        mesh=mesh,
        in_specs=(
            P("ctx", "tp"),
            P("ctx", "tp"),
            P("ctx", "tp"),
            P("ctx", "tp"),
            P("tp", None),
            P("tp", None),
        ),
        out_specs=(P("ctx", "tp"), P("ctx", "tp"), P("ctx", "tp")),
        check_vma=False,
    )
```

```python
import functools
import math

import jax
import jax.numpy as jnp
from jax import lax
from jax.experimental import pallas as pl
from jax.experimental.pallas import tpu as pltpu
from jax.sharding import PartitionSpec as P

LEVELS = 3
KEYS_SEG = 1024
MESH = pl.DeviceIdType.MESH
NEGATIVE_FILL = -1e30
CHUNKS = 4
SUB = 256
F32 = jnp.float32
BF16 = jnp.bfloat16


def nt(a, b):
    return lax.dot_general(a, b, (((1,), (1,)), ((), ())), preferred_element_type=F32)


def tn(a, b):
    return lax.dot_general(a, b, (((0,), (0,)), ((), ())), preferred_element_type=F32)


def owner_turns(group, wide, own_slot):
    turns = group // 4
    listed = [(turns, turns - 1, own_slot < group, own_slot)]
    for j in range(1, turns):
        listed.append((j, j - 1, own_slot <= 4 * j + 1, own_slot))
    if wide:
        listed.append((0, turns, own_slot < 2, group + own_slot))
    return listed


def kernel(
    n, q_ref, k_ref, v_ref, og_ref, w_hbm, off_ref, dq_ref, part_buf,
    w_buf, og_buf, stage, grad_buf, q_buf, g_buf, kv_buf, s_buf, p_buf, ds_buf, wl_buf,
    dkv_acc, dkv_low, dq_low,
    w_sem, og_sem, stage_sem, og_send, og_recv, fw_send, fw_recv, pair_send, pair_recv,
    kv_send, kv_recv, q_send, q_recv, g_send, g_recv,
    dq_send, dq_recv, part_send, part_recv,
):
    tok, width = q_ref.shape
    heads = off_ref.shape[0]
    dim = width // heads
    feats = og_ref.shape[1]
    group = min(KEYS_SEG * 2 ** (LEVELS - 1), tok * n) // tok
    pairs = group // 2
    rows = 2 * tok
    quads = n // 4
    turns = group // 4
    wide = n > group
    me = lax.axis_index("ctx")
    tp = lax.axis_index("tp")
    quad, head = me // 4, me % 4
    start = (4 * quad) % group
    straddle = start == 0
    u_block = (me + n - 2) % n
    own_group, own_slot = u_block // group, u_block % group
    first_group = ((4 * quad + n - 2) % n) // group
    core_peer = tp + 1 - 2 * (tp % 2)
    y_peer = (tp + 2) % 4
    far_peer = (core_peer + 2) % 4

    def move(src, dst, send, recv, target):
        @pl.when(target != me)
        def _():
            pltpu.make_async_remote_copy(
                src_ref=src, dst_ref=dst, send_sem=send, recv_sem=recv,
                device_id={"ctx": target}, device_id_type=MESH,
            ).start()

        @pl.when(target == me)
        def _():
            pltpu.make_async_copy(src, dst, recv).start()

    def sent(src, send, target):
        @pl.when(target != me)
        def _():
            pltpu.make_async_copy(src, src, send).wait()

    def arrived(dst, recv):
        pltpu.make_async_copy(dst, dst, recv).wait()

    def block(index, size):
        return pl.ds(pl.multiple_of(index * size, size), size)

    staged = []
    for kind, ref in enumerate((k_ref, v_ref, q_ref)):
        for h in range(4):
            staged.append(pltpu.make_async_copy(
                ref.at[:, pl.ds(h * dim, dim)], stage.at[kind, h], stage_sem.at[kind, h]
            ))
            staged[-1].start()
    w_copy = pltpu.make_async_copy(w_hbm, w_buf, w_sem)
    w_copy.start()
    og_copy = pltpu.make_async_copy(og_ref, og_buf.at[3], og_sem)
    og_copy.start()

    barrier = pltpu.get_barrier_semaphore()
    for step in range(1, n):
        pl.semaphore_signal(
            barrier, inc=1, device_id={"ctx": (me + step) % n}, device_id_type=MESH
        )
    for peer in (core_peer, y_peer):
        pl.semaphore_signal(barrier, inc=1, device_id={"tp": peer}, device_id_type=MESH)
    pl.semaphore_wait(barrier, n + 1)

    def tp_copy(src, dst, send, recv, peer):
        return pltpu.make_async_remote_copy(
            src_ref=src, dst_ref=dst, send_sem=send, recv_sem=recv,
            device_id={"tp": peer}, device_id_type=MESH,
        )

    piece = feats // CHUNKS
    for c in range(CHUNKS):
        part = pl.ds(c * piece, piece)
        tp_copy(
            og_ref.at[:, part], og_buf.at[1, :, part], og_send.at[c], og_recv.at[c], y_peer
        ).start()
    tp_copy(og_ref, og_buf.at[0], pair_send, pair_recv, core_peer).start()

    for copy in staged:
        copy.wait()
    turn_list = owner_turns(group, wide, own_slot)

    def send_kv(act, kind, entry):
        j, at, needed, slot = entry

        @pl.when(needed)
        def _():
            to_quad = (own_group * turns + j) % quads
            for h in range(4):
                act(kind, at, h, slot, 4 * to_quad + h)

    def start_kv(kind, at, h, slot, target):
        move(
            stage.at[kind, h], kv_buf.at[kind, block(slot, tok)],
            kv_send.at[kind, at, h], kv_recv.at[kind, slot], target,
        )

    send_kv(start_kv, 0, turn_list[0])
    for h in range(4):
        move(
            stage.at[2, h], q_buf.at[block(head, tok)],
            q_send.at[h], q_recv.at[head], 4 * quad + h,
        )
    for entry in turn_list[1:]:
        send_kv(start_kv, 0, entry)
    send_kv(start_kv, 1, turn_list[0])

    dkv_acc[...] = jnp.zeros_like(dkv_acc)

    w_copy.wait()
    og_copy.wait()

    def w_part(shard, c):
        return w_buf[:, pl.ds(pl.multiple_of(shard * feats + c * piece, piece), piece)]

    total = nt(og_buf[3], w_buf[:, block(tp, feats)])
    arrived(og_buf.at[0], pair_recv)
    total += nt(og_buf[0], w_buf[:, block(core_peer, feats)])
    for c in range(CHUNKS):
        part = pl.ds(c * piece, piece)
        arrived(og_buf.at[1, :, part], og_recv.at[c])
        tp_copy(
            og_buf.at[1, :, part], og_buf.at[2, :, part], fw_send.at[c], fw_recv.at[c], core_peer
        ).start()
        total += nt(og_buf[1, :, part], w_part(y_peer, c))
    for c in range(CHUNKS):
        part = pl.ds(c * piece, piece)
        arrived(og_buf.at[2, :, part], fw_recv.at[c])
        total += nt(og_buf[2, :, part], w_part(far_peer, c))
    for h in range(4):
        grad_buf[h] = total[:, h * dim:(h + 1) * dim].astype(BF16)
        move(
            grad_buf.at[h], g_buf.at[block(head, tok)],
            g_send.at[h], g_recv.at[head], 4 * quad + h,
        )

    for entry in turn_list[1:]:
        send_kv(start_kv, 1, entry)

    def wait_pair(kind, pair):
        for b in range(2):
            slot = 2 * pair + b
            arrived(kv_buf.at[kind, block(slot, tok)], kv_recv.at[kind, slot])

    for b in range(4):
        arrived(q_buf.at[block(b, tok)], q_recv.at[b])

    odd1, odd2 = off_ref[head, 1], off_ref[head, 2]
    key_row = lax.broadcasted_iota(jnp.int32, (8, rows), 0)
    query_col = lax.broadcasted_iota(jnp.int32, (8, rows), 1)
    both1 = ((key_row % 2 == odd1) & (query_col % 2 == odd1)).astype(F32)
    both2 = ((key_row % 4 == odd2) & (query_col % 4 == odd2)).astype(F32)
    sub_row = lax.broadcasted_iota(jnp.int32, (SUB, rows), 0)
    sub_col = lax.broadcasted_iota(jnp.int32, (SUB, rows), 1)
    score_scale = 1.0 / math.sqrt(dim)
    to_exp2 = score_scale / math.log(2.0)
    first_pair = jnp.where(straddle, 0, start // 2 - 1)
    first_base = jnp.where(straddle, pairs, 0) if wide else 0
    last_pair = jnp.where(straddle, pairs - 1, start // 2)
    early = jnp.where(straddle, 1, 0)
    halves = [(early, first_pair, first_base), (1 - early, last_pair, 0)]

    def arrival(turn, step):
        return step if turn == 0 else jnp.where(straddle, step, last_pair - 1 - step)

    def wait_new(turn, kind, kp):
        if turn == 0:
            wait_pair(kind, first_base + kp)
        else:
            fresh = kp > first_pair
            if wide:
                fresh = fresh | straddle
            pl.when(fresh)(functools.partial(wait_pair, kind, kp))

    def folded(values):
        return values.reshape(values.shape[0] // 8, 8, values.shape[1])

    logs = []
    for turn, (half, at_pair, base) in enumerate(halves):
        queries = q_buf[block(half, rows), :]

        def score_tile(kp, state, causal, turn=turn, at_pair=at_pair, base=base, queries=queries):
            wait_new(turn, 0, kp)
            same0 = jnp.where(at_pair // 2 == kp // 2, 1.0, 0.0)
            same1 = jnp.where(at_pair // 4 == kp // 4, 1.0, 0.0)
            count = same0 + same1 * both1 + both2
            bias = jnp.where(
                count > 2.5, math.log2(3.0),
                jnp.where(count > 1.5, 1.0, jnp.where(count > 0.5, 0.0, NEGATIVE_FILL)),
            )
            top, den = state
            for s in range(rows // SUB):
                keys = kv_buf[0, pl.ds(pl.multiple_of((base + kp) * rows + s * SUB, SUB), SUB), :]
                scores = folded(nt(keys, queries) * to_exp2) + bias[None]
                if causal:
                    scores = scores.reshape(SUB, rows)
                    scores = folded(jnp.where(sub_row + s * SUB <= sub_col, scores, NEGATIVE_FILL))
                s_buf[turn, kp, s * SUB:(s + 1) * SUB, :] = scores.reshape(SUB, rows)
                new_top = jnp.maximum(top, jnp.max(scores, axis=0))
                den = den * jnp.exp2(top - new_top) + jnp.sum(
                    jnp.exp2(scores - new_top[None]), axis=0
                )
                top = new_top
            return top, den

        state = (jnp.full((8, rows), NEGATIVE_FILL, F32), jnp.zeros((8, rows), F32))
        state = score_tile(at_pair, state, True)
        top, den = lax.fori_loop(
            0, at_pair,
            lambda step, state, turn=turn, tile=score_tile: tile(arrival(turn, step), state, False),
            state,
        )
        row_top = jnp.max(top, axis=0, keepdims=True)
        row_total = jnp.sum(den * jnp.exp2(top - row_top), axis=0, keepdims=True)
        logs.append(row_top + jnp.log2(row_total))

    part_at = jnp.where(straddle, turns, start // 4) - 1

    def slot_owner(slot):
        return (first_group * group + slot + 2) % n

    def send_slot(kind, slot, owner, at):
        move(
            dkv_low.at[kind, block(slot, tok)], part_buf.at[kind, at, head],
            part_send.at[kind, slot], part_recv.at[kind, at, head], owner,
        )

    def round_pair(kind, kp):
        done = dkv_acc[kind, block(kp, rows), :]
        if kind == 0:
            done = done * score_scale
        dkv_low[kind, block(kp, rows), :] = done.astype(BF16)

    def send_pair(kind, kp):
        round_pair(kind, kp)
        for b in range(2):
            slot = 2 * kp + b
            send_slot(kind, slot, slot_owner(slot), part_at)

    def leaving(turn, step):
        if turn == 0:
            return step
        return (step + jnp.where(straddle, 1, 0)) % (halves[1][1] + 1)

    zero = jnp.zeros((8, rows), F32)
    for turn, (half, at_pair, base) in enumerate(halves):
        for b in range(2):
            arrived(g_buf.at[block(2 * half + b, tok)], g_recv.at[2 * half + b])
        queries = q_buf[block(half, rows), :]
        grads = g_buf[block(half, rows), :]

        def weigh_body(step, num, turn=turn, base=base, grads=grads):
            kp = leaving(turn, step)
            for s in range(rows // SUB):
                here = slice(s * SUB, (s + 1) * SUB)
                weight = jnp.exp2(s_buf[turn, kp, here, :] - logs[turn])
                s_buf[turn, kp, here, :] = weight
                wl_buf[here, :] = weight.astype(BF16)
            place = block(base + kp, rows)
            dkv_acc[1, place, :] += jnp.dot(wl_buf[...], grads, preferred_element_type=F32)
            if turn == 1:
                send_pair(1, kp)
            wait_new(turn, 1, kp)
            for s in range(rows // SUB):
                here = slice(s * SUB, (s + 1) * SUB)
                vals = kv_buf[1, pl.ds(pl.multiple_of((base + kp) * rows + s * SUB, SUB), SUB), :]
                prob = nt(vals, grads)
                p_buf[kp, here, :] = prob
                num = num + jnp.sum(folded(s_buf[turn, kp, here, :] * prob), axis=0)
            return num

        num = lax.fori_loop(0, at_pair + 1, weigh_body, zero)
        delta = jnp.sum(num, axis=0, keepdims=True)

        def grad_body(step, total, turn=turn, base=base, queries=queries, delta=delta):
            kp = leaving(turn, step)
            for s in range(rows // SUB):
                here = slice(s * SUB, (s + 1) * SUB)
                ds_buf[here, :] = (
                    s_buf[turn, kp, here, :] * (p_buf[kp, here, :] - delta)
                ).astype(BF16)
            place = block(base + kp, rows)
            score_grad = ds_buf[...]
            dkv_acc[0, place, :] += jnp.dot(score_grad, queries, preferred_element_type=F32)
            if turn == 1:
                send_pair(0, kp)
            return total + tn(kv_buf[0, place, :], score_grad)

        total = lax.fori_loop(0, at_pair + 1, grad_body, jnp.zeros((dim, rows), F32))
        dq_low[block(half, rows), :] = (total * score_scale).T.astype(BF16)
        for b in range(2):
            move(
                dq_low.at[block(2 * half + b, tok)], dq_ref.at[head],
                dq_send.at[2 * half + b], dq_recv.at[head], 4 * quad + 2 * half + b,
            )
    if wide:
        @pl.when(straddle)
        def _():
            for kind in range(2):
                round_pair(kind, pairs)
                for b in range(2):
                    send_slot(kind, group + b, (4 * quad + b + 2) % n, turns)

    for j, at, needed, slot in turn_list:
        @pl.when(needed)
        def _(at=at):
            for kind in range(2):
                for h in range(4):
                    arrived(part_buf.at[kind, at, h], part_recv.at[kind, at, h])
    for h in range(4):
        arrived(dq_ref.at[h], dq_recv.at[h])

    for c in range(CHUNKS):
        part = pl.ds(c * piece, piece)
        pltpu.make_async_copy(og_ref.at[:, part], og_ref.at[:, part], og_send.at[c]).wait()
        pltpu.make_async_copy(og_ref.at[:, part], og_ref.at[:, part], fw_send.at[c]).wait()
    pltpu.make_async_copy(og_ref, og_ref, pair_send).wait()
    for h in range(4):
        sent(stage.at[2, h], q_send.at[h], 4 * quad + h)
        sent(grad_buf.at[h], g_send.at[h], 4 * quad + h)
        sent(dq_low.at[pl.ds(h * tok, tok)], dq_send.at[h], 4 * quad + h)

    def kv_sent(kind, at, h, slot, target):
        sent(stage.at[kind, h], kv_send.at[kind, at, h], target)

    for kind in range(2):
        for entry in turn_list:
            send_kv(kv_sent, kind, entry)

    def slot_sent(slot):
        owner = slot_owner(slot) if slot < group else (4 * quad + slot - group + 2) % n
        for kind in range(2):
            sent(dkv_low.at[kind, pl.ds(slot * tok, tok)], part_send.at[kind, slot], owner)

    for slot in range(group + 2 * wide):
        needed = straddle | (slot <= start + 1) if slot < group else straddle
        pl.when(needed)(functools.partial(slot_sent, slot))


def add_kernel(n, group, dq_ref, part_ref, dq_out, dk_out, dv_out):
    own_slot = ((lax.axis_index("ctx") + n - 2) % n) % group
    dim = dq_ref.shape[2]
    for h in range(4):
        here = slice(h * dim, (h + 1) * dim)
        dq_out[:, here] = dq_ref[h]
        for kind, out in ((0, dk_out), (1, dv_out)):
            total = None
            for j, at, needed, slot in owner_turns(group, n > group, own_slot):
                part = part_ref[kind, at, h].astype(F32)
                total = part if total is None else total + jnp.where(needed, part, 0.0)
            out[:, here] = total.astype(BF16)


def local(queries, keys, values, out_grad, w_out, offsets):
    n = lax.axis_size("ctx")
    tok, width = queries.shape
    heads = offsets.shape[0]
    dim = width // heads
    feats = out_grad.shape[1]
    group = min(KEYS_SEG * 2 ** (LEVELS - 1), tok * n) // tok
    assert heads == 4 and tok * 4 == KEYS_SEG and lax.axis_size("tp") == 4
    assert n % group == 0 and group % 4 == 0
    pairs, rows, turns = group // 2, 2 * tok, group // 4
    wide = n > group
    slots = group + 2 * wide
    kinds = turns + wide
    dma = pltpu.SemaphoreType.DMA
    out = jax.ShapeDtypeStruct((tok, width), BF16)
    hbm = pl.BlockSpec(memory_space=pl.ANY)
    dq_raw, parts = pl.pallas_call(
        functools.partial(kernel, n),
        out_shape=(
            jax.ShapeDtypeStruct((4, tok, dim), BF16),
            jax.ShapeDtypeStruct((2, kinds, 4, tok, dim), BF16),
        ),
        in_specs=[hbm] * 5 + [pl.BlockSpec(memory_space=pltpu.SMEM)],
        out_specs=(hbm, hbm),
        scratch_shapes=[
            pltpu.VMEM(w_out.shape, BF16),
            pltpu.VMEM((4, tok, feats), BF16),
            pltpu.VMEM((3, 4, tok, dim), BF16),
            pltpu.VMEM((4, tok, dim), BF16),
            pltpu.VMEM((4 * tok, dim), BF16),
            pltpu.VMEM((4 * tok, dim), BF16),
            pltpu.VMEM((2, slots * tok, dim), BF16),
            pltpu.VMEM((2, pairs, rows, rows), F32),
            pltpu.VMEM((pairs, rows, rows), F32),
            pltpu.VMEM((rows, rows), BF16),
            pltpu.VMEM((rows, rows), BF16),
            pltpu.VMEM((2, slots * tok, dim), F32),
            pltpu.VMEM((2, slots * tok, dim), BF16),
            pltpu.VMEM((4 * tok, dim), BF16),
            dma, dma, dma((3, 4)), dma((CHUNKS,)), dma((CHUNKS,)), dma((CHUNKS,)), dma((CHUNKS,)), dma, dma,
            dma((2, kinds, 4)), dma((2, slots)), dma((4,)), dma((4,)), dma((4,)), dma((4,)),
            dma((4,)), dma((4,)), dma((2, slots)), dma((2, kinds, 4)),
        ],
        compiler_params=pltpu.CompilerParams(
            collective_id=0, has_side_effects=True, vmem_limit_bytes=56 * 1024 * 1024
        ),
        cost_estimate=pl.CostEstimate(
            flops=5 * 10 * rows * rows * dim + 2 * tok * width * feats * 4,
            bytes_accessed=2 * (w_out.size + 8 * tok * width), transcendentals=5 * rows * rows,
        ),
    )(queries, keys, values, out_grad, w_out, offsets)
    steps = 2
    flat = pl.BlockSpec((tok // steps, width), lambda i: (i, 0))
    return pl.pallas_call(
        functools.partial(add_kernel, n, group),
        grid=(steps,),
        out_shape=(out, out, out),
        in_specs=[
            pl.BlockSpec((4, tok // steps, dim), lambda i: (0, i, 0)),
            pl.BlockSpec((2, kinds, 4, tok // steps, dim), lambda i: (0, 0, 0, i, 0)),
        ],
        out_specs=(flat, flat, flat),
        compiler_params=pltpu.CompilerParams(vmem_limit_bytes=60 * 1024 * 1024),
    )(dq_raw, parts)


def solution(mesh):
    return jax.shard_map(
        local,
        mesh=mesh,
        in_specs=(
            P("ctx", "tp"),
            P("ctx", "tp"),
            P("ctx", "tp"),
            P("ctx", "tp"),
            P("tp", None),
            P("tp", None),
        ),
        out_specs=(P("ctx", "tp"), P("ctx", "tp"), P("ctx", "tp")),
        check_vma=False,
    )
```

```python
import functools
import math

import jax
import jax.numpy as jnp
from jax import lax
from jax.experimental import pallas as pl
from jax.experimental.pallas import tpu as pltpu
from jax.sharding import PartitionSpec as P

LEVELS = 3
KEYS_SEG = 1024
MESH = pl.DeviceIdType.MESH
NEGATIVE_FILL = -1e30
CHUNKS = 4
SUB = 256
F32 = jnp.float32
BF16 = jnp.bfloat16


def nt(a, b):
    return lax.dot_general(a, b, (((1,), (1,)), ((), ())), preferred_element_type=F32)


def tn(a, b):
    return lax.dot_general(a, b, (((0,), (0,)), ((), ())), preferred_element_type=F32)


def owner_turns(group, wide, own_slot):
    turns = group // 4
    listed = [(turns, turns - 1, own_slot < group, own_slot)]
    for j in range(1, turns):
        listed.append((j, j - 1, own_slot <= 4 * j + 1, own_slot))
    if wide:
        listed.append((0, turns, own_slot < 2, group + own_slot))
    return listed


def kernel(
    n, q_ref, k_ref, v_ref, og_ref, w_hbm, off_ref, dq_ref, part_buf,
    w_buf, og_buf, stage, grad_buf, q_buf, g_buf, kv_buf, s_buf, p_buf, ds_buf, wl_buf, turned_buf,
    dkv_acc, dkv_low, dq_low,
    w_sem, og_sem, stage_sem, og_send, og_recv, fw_send, fw_recv, pair_send, pair_recv,
    kv_send, kv_recv, q_send, q_recv, g_send, g_recv,
    dq_send, dq_recv, part_send, part_recv,
):
    tok, width = q_ref.shape
    heads = off_ref.shape[0]
    dim = width // heads
    feats = og_ref.shape[1]
    group = min(KEYS_SEG * 2 ** (LEVELS - 1), tok * n) // tok
    pairs = group // 2
    rows = 2 * tok
    quads = n // 4
    turns = group // 4
    wide = n > group
    me = lax.axis_index("ctx")
    tp = lax.axis_index("tp")
    quad, head = me // 4, me % 4
    start = (4 * quad) % group
    straddle = start == 0
    u_block = (me + n - 2) % n
    own_group, own_slot = u_block // group, u_block % group
    first_group = ((4 * quad + n - 2) % n) // group
    core_peer = tp + 1 - 2 * (tp % 2)
    y_peer = (tp + 2) % 4
    far_peer = (core_peer + 2) % 4

    def move(src, dst, send, recv, target):
        @pl.when(target != me)
        def _():
            pltpu.make_async_remote_copy(
                src_ref=src, dst_ref=dst, send_sem=send, recv_sem=recv,
                device_id={"ctx": target}, device_id_type=MESH,
            ).start()

        @pl.when(target == me)
        def _():
            pltpu.make_async_copy(src, dst, recv).start()

    def sent(src, send, target):
        @pl.when(target != me)
        def _():
            pltpu.make_async_copy(src, src, send).wait()

    def arrived(dst, recv):
        pltpu.make_async_copy(dst, dst, recv).wait()

    def block(index, size):
        return pl.ds(pl.multiple_of(index * size, size), size)

    staged = []
    for kind, ref in enumerate((k_ref, v_ref, q_ref)):
        for h in range(4):
            staged.append(pltpu.make_async_copy(
                ref.at[:, pl.ds(h * dim, dim)], stage.at[kind, h], stage_sem.at[kind, h]
            ))
            staged[-1].start()
    w_copy = pltpu.make_async_copy(w_hbm, w_buf, w_sem)
    w_copy.start()
    og_copy = pltpu.make_async_copy(og_ref, og_buf.at[3], og_sem)
    og_copy.start()

    barrier = pltpu.get_barrier_semaphore()
    for step in range(1, n):
        pl.semaphore_signal(
            barrier, inc=1, device_id={"ctx": (me + step) % n}, device_id_type=MESH
        )
    for peer in (core_peer, y_peer):
        pl.semaphore_signal(barrier, inc=1, device_id={"tp": peer}, device_id_type=MESH)
    pl.semaphore_wait(barrier, n + 1)

    def tp_copy(src, dst, send, recv, peer):
        return pltpu.make_async_remote_copy(
            src_ref=src, dst_ref=dst, send_sem=send, recv_sem=recv,
            device_id={"tp": peer}, device_id_type=MESH,
        )

    piece = feats // CHUNKS
    for c in range(CHUNKS):
        part = pl.ds(c * piece, piece)
        tp_copy(
            og_ref.at[:, part], og_buf.at[1, :, part], og_send.at[c], og_recv.at[c], y_peer
        ).start()
    tp_copy(og_ref, og_buf.at[0], pair_send, pair_recv, core_peer).start()

    for copy in staged:
        copy.wait()
    turn_list = owner_turns(group, wide, own_slot)

    def send_kv(act, kind, entry):
        j, at, needed, slot = entry

        @pl.when(needed)
        def _():
            to_quad = (own_group * turns + j) % quads
            for h in range(4):
                act(kind, at, h, slot, 4 * to_quad + h)

    def start_kv(kind, at, h, slot, target):
        move(
            stage.at[kind, h], kv_buf.at[kind, block(slot, tok)],
            kv_send.at[kind, at, h], kv_recv.at[kind, slot], target,
        )

    send_kv(start_kv, 0, turn_list[0])
    for h in range(4):
        move(
            stage.at[2, h], q_buf.at[block(head, tok)],
            q_send.at[h], q_recv.at[head], 4 * quad + h,
        )
    for entry in turn_list[1:]:
        send_kv(start_kv, 0, entry)
    send_kv(start_kv, 1, turn_list[0])

    dkv_acc[...] = jnp.zeros_like(dkv_acc)

    w_copy.wait()
    og_copy.wait()

    def w_part(shard, c):
        return w_buf[:, pl.ds(pl.multiple_of(shard * feats + c * piece, piece), piece)]

    total = nt(w_buf[:, block(tp, feats)], og_buf[3])
    arrived(og_buf.at[0], pair_recv)
    total += nt(w_buf[:, block(core_peer, feats)], og_buf[0])
    for c in range(CHUNKS):
        part = pl.ds(c * piece, piece)
        arrived(og_buf.at[1, :, part], og_recv.at[c])
        tp_copy(
            og_buf.at[1, :, part], og_buf.at[2, :, part], fw_send.at[c], fw_recv.at[c], core_peer
        ).start()
        total += nt(w_part(y_peer, c), og_buf[1, :, part])
    for c in range(CHUNKS):
        part = pl.ds(c * piece, piece)
        arrived(og_buf.at[2, :, part], fw_recv.at[c])
        total += nt(w_part(far_peer, c), og_buf[2, :, part])
    for h in range(4):
        grad_buf[h] = total[h * dim:(h + 1) * dim, :].T.astype(BF16)
        move(
            grad_buf.at[h], g_buf.at[block(head, tok)],
            g_send.at[h], g_recv.at[head], 4 * quad + h,
        )

    for entry in turn_list[1:]:
        send_kv(start_kv, 1, entry)

    def wait_pair(kind, pair):
        for b in range(2):
            slot = 2 * pair + b
            arrived(kv_buf.at[kind, block(slot, tok)], kv_recv.at[kind, slot])

    for b in range(4):
        arrived(q_buf.at[block(b, tok)], q_recv.at[b])

    odd1, odd2 = off_ref[head, 1], off_ref[head, 2]
    key_row = lax.broadcasted_iota(jnp.int32, (8, rows), 0)
    query_col = lax.broadcasted_iota(jnp.int32, (8, rows), 1)
    both1 = ((key_row % 2 == odd1) & (query_col % 2 == odd1)).astype(F32)
    both2 = ((key_row % 4 == odd2) & (query_col % 4 == odd2)).astype(F32)
    sub_row = lax.broadcasted_iota(jnp.int32, (SUB, rows), 0)
    sub_col = lax.broadcasted_iota(jnp.int32, (SUB, rows), 1)
    score_scale = 1.0 / math.sqrt(dim)
    to_exp2 = score_scale / math.log(2.0)
    first_pair = jnp.where(straddle, 0, start // 2 - 1)
    first_base = jnp.where(straddle, pairs, 0) if wide else 0
    last_pair = jnp.where(straddle, pairs - 1, start // 2)
    early = jnp.where(straddle, 1, 0)
    halves = [(early, first_pair, first_base), (1 - early, last_pair, 0)]

    def arrival(turn, step):
        return step if turn == 0 else jnp.where(straddle, step, last_pair - 1 - step)

    def wait_new(turn, kind, kp):
        if turn == 0:
            wait_pair(kind, first_base + kp)
        else:
            fresh = kp > first_pair
            if wide:
                fresh = fresh | straddle
            pl.when(fresh)(functools.partial(wait_pair, kind, kp))

    def folded(values):
        return values.reshape(values.shape[0] // 8, 8, values.shape[1])

    logs = []
    for turn, (half, at_pair, base) in enumerate(halves):
        queries = q_buf[block(half, rows), :]

        turned_buf[...] = queries.T

        def score_tile(kp, state, causal, turn=turn, at_pair=at_pair, base=base, queries=queries):
            wait_new(turn, 0, kp)
            same0 = jnp.where(at_pair // 2 == kp // 2, 1.0, 0.0)
            same1 = jnp.where(at_pair // 4 == kp // 4, 1.0, 0.0)
            count = same0 + same1 * both1 + both2
            bias = jnp.where(
                count > 2.5, math.log2(3.0),
                jnp.where(count > 1.5, 1.0, jnp.where(count > 0.5, 0.0, NEGATIVE_FILL)),
            )
            top, den = state
            for s in range(rows // SUB):
                keys = kv_buf[0, pl.ds(pl.multiple_of((base + kp) * rows + s * SUB, SUB), SUB), :]
                scores = folded(jnp.dot(keys, turned_buf[...], preferred_element_type=F32) * to_exp2) + bias[None]
                if causal:
                    scores = scores.reshape(SUB, rows)
                    scores = folded(jnp.where(sub_row + s * SUB <= sub_col, scores, NEGATIVE_FILL))
                s_buf[turn, kp, s * SUB:(s + 1) * SUB, :] = scores.reshape(SUB, rows)
                new_top = jnp.maximum(top, jnp.max(scores, axis=0))
                den = den * jnp.exp2(top - new_top) + jnp.sum(
                    jnp.exp2(scores - new_top[None]), axis=0
                )
                top = new_top
            return top, den

        state = (jnp.full((8, rows), NEGATIVE_FILL, F32), jnp.zeros((8, rows), F32))
        state = score_tile(at_pair, state, True)
        top, den = lax.fori_loop(
            0, at_pair,
            lambda step, state, turn=turn, tile=score_tile: tile(arrival(turn, step), state, False),
            state,
        )
        row_top = jnp.max(top, axis=0, keepdims=True)
        row_total = jnp.sum(den * jnp.exp2(top - row_top), axis=0, keepdims=True)
        logs.append(row_top + jnp.log2(row_total))

    part_at = jnp.where(straddle, turns, start // 4) - 1

    def slot_owner(slot):
        return (first_group * group + slot + 2) % n

    def send_slot(kind, slot, owner, at):
        move(
            dkv_low.at[kind, block(slot, tok)], part_buf.at[kind, at, head],
            part_send.at[kind, slot], part_recv.at[kind, at, head], owner,
        )

    def round_pair(kind, kp):
        done = dkv_acc[kind, block(kp, rows), :]
        if kind == 0:
            done = done * score_scale
        dkv_low[kind, block(kp, rows), :] = done.astype(BF16)

    def send_pair(kind, kp):
        round_pair(kind, kp)
        for b in range(2):
            slot = 2 * kp + b
            send_slot(kind, slot, slot_owner(slot), part_at)

    def leaving(turn, step):
        if turn == 0:
            return step
        return (step + jnp.where(straddle, 1, 0)) % (halves[1][1] + 1)

    zero = jnp.zeros((8, rows), F32)
    for turn, (half, at_pair, base) in enumerate(halves):
        for b in range(2):
            arrived(g_buf.at[block(2 * half + b, tok)], g_recv.at[2 * half + b])
        queries = q_buf[block(half, rows), :]
        grads = g_buf[block(half, rows), :]

        turned_buf[...] = grads.T

        def weigh_body(step, num, turn=turn, base=base, grads=grads):
            kp = leaving(turn, step)
            for s in range(rows // SUB):
                here = slice(s * SUB, (s + 1) * SUB)
                weight = jnp.exp2(s_buf[turn, kp, here, :] - logs[turn])
                s_buf[turn, kp, here, :] = weight
                wl_buf[here, :] = weight.astype(BF16)
            place = block(base + kp, rows)
            dkv_acc[1, place, :] += jnp.dot(wl_buf[...], grads, preferred_element_type=F32)
            if turn == 1:
                send_pair(1, kp)
            wait_new(turn, 1, kp)
            for s in range(rows // SUB):
                here = slice(s * SUB, (s + 1) * SUB)
                vals = kv_buf[1, pl.ds(pl.multiple_of((base + kp) * rows + s * SUB, SUB), SUB), :]
                prob = jnp.dot(vals, turned_buf[...], preferred_element_type=F32)
                p_buf[kp, here, :] = prob
                num = num + jnp.sum(folded(s_buf[turn, kp, here, :] * prob), axis=0)
            return num

        num = lax.fori_loop(0, at_pair + 1, weigh_body, zero)
        delta = jnp.sum(num, axis=0, keepdims=True)

        def grad_body(step, total, turn=turn, base=base, queries=queries, delta=delta):
            kp = leaving(turn, step)
            for s in range(rows // SUB):
                here = slice(s * SUB, (s + 1) * SUB)
                ds_buf[here, :] = (
                    s_buf[turn, kp, here, :] * (p_buf[kp, here, :] - delta)
                ).astype(BF16)
            place = block(base + kp, rows)
            score_grad = ds_buf[...]
            dkv_acc[0, place, :] += jnp.dot(score_grad, queries, preferred_element_type=F32)
            if turn == 1:
                send_pair(0, kp)
            return total + tn(kv_buf[0, place, :], score_grad)

        total = lax.fori_loop(0, at_pair + 1, grad_body, jnp.zeros((dim, rows), F32))
        dq_low[block(half, rows), :] = (total * score_scale).T.astype(BF16)
        for b in range(2):
            move(
                dq_low.at[block(2 * half + b, tok)], dq_ref.at[head],
                dq_send.at[2 * half + b], dq_recv.at[head], 4 * quad + 2 * half + b,
            )
    if wide:
        @pl.when(straddle)
        def _():
            for kind in range(2):
                round_pair(kind, pairs)
                for b in range(2):
                    send_slot(kind, group + b, (4 * quad + b + 2) % n, turns)

    for j, at, needed, slot in turn_list:
        @pl.when(needed)
        def _(at=at):
            for kind in range(2):
                for h in range(4):
                    arrived(part_buf.at[kind, at, h], part_recv.at[kind, at, h])
    for h in range(4):
        arrived(dq_ref.at[h], dq_recv.at[h])

    for c in range(CHUNKS):
        part = pl.ds(c * piece, piece)
        pltpu.make_async_copy(og_ref.at[:, part], og_ref.at[:, part], og_send.at[c]).wait()
        pltpu.make_async_copy(og_ref.at[:, part], og_ref.at[:, part], fw_send.at[c]).wait()
    pltpu.make_async_copy(og_ref, og_ref, pair_send).wait()
    for h in range(4):
        sent(stage.at[2, h], q_send.at[h], 4 * quad + h)
        sent(grad_buf.at[h], g_send.at[h], 4 * quad + h)
        sent(dq_low.at[pl.ds(h * tok, tok)], dq_send.at[h], 4 * quad + h)

    def kv_sent(kind, at, h, slot, target):
        sent(stage.at[kind, h], kv_send.at[kind, at, h], target)

    for kind in range(2):
        for entry in turn_list:
            send_kv(kv_sent, kind, entry)

    def slot_sent(slot):
        owner = slot_owner(slot) if slot < group else (4 * quad + slot - group + 2) % n
        for kind in range(2):
            sent(dkv_low.at[kind, pl.ds(slot * tok, tok)], part_send.at[kind, slot], owner)

    for slot in range(group + 2 * wide):
        needed = straddle | (slot <= start + 1) if slot < group else straddle
        pl.when(needed)(functools.partial(slot_sent, slot))


def add_kernel(n, group, dq_ref, part_ref, dq_out, dk_out, dv_out):
    own_slot = ((lax.axis_index("ctx") + n - 2) % n) % group
    dim = dq_ref.shape[2]
    for h in range(4):
        here = slice(h * dim, (h + 1) * dim)
        dq_out[:, here] = dq_ref[h]
        for kind, out in ((0, dk_out), (1, dv_out)):
            total = None
            for j, at, needed, slot in owner_turns(group, n > group, own_slot):
                part = part_ref[kind, at, h].astype(F32)
                total = part if total is None else total + jnp.where(needed, part, 0.0)
            out[:, here] = total.astype(BF16)


def local(queries, keys, values, out_grad, w_out, offsets):
    n = lax.axis_size("ctx")
    tok, width = queries.shape
    heads = offsets.shape[0]
    dim = width // heads
    feats = out_grad.shape[1]
    group = min(KEYS_SEG * 2 ** (LEVELS - 1), tok * n) // tok
    assert heads == 4 and tok * 4 == KEYS_SEG and lax.axis_size("tp") == 4
    assert n % group == 0 and group % 4 == 0
    pairs, rows, turns = group // 2, 2 * tok, group // 4
    wide = n > group
    slots = group + 2 * wide
    kinds = turns + wide
    dma = pltpu.SemaphoreType.DMA
    out = jax.ShapeDtypeStruct((tok, width), BF16)
    hbm = pl.BlockSpec(memory_space=pl.ANY)
    dq_raw, parts = pl.pallas_call(
        functools.partial(kernel, n),
        out_shape=(
            jax.ShapeDtypeStruct((4, tok, dim), BF16),
            jax.ShapeDtypeStruct((2, kinds, 4, tok, dim), BF16),
        ),
        in_specs=[hbm] * 5 + [pl.BlockSpec(memory_space=pltpu.SMEM)],
        out_specs=(hbm, hbm),
        scratch_shapes=[
            pltpu.VMEM(w_out.shape, BF16),
            pltpu.VMEM((4, tok, feats), BF16),
            pltpu.VMEM((3, 4, tok, dim), BF16),
            pltpu.VMEM((4, tok, dim), BF16),
            pltpu.VMEM((4 * tok, dim), BF16),
            pltpu.VMEM((4 * tok, dim), BF16),
            pltpu.VMEM((2, slots * tok, dim), BF16),
            pltpu.VMEM((2, pairs, rows, rows), F32),
            pltpu.VMEM((pairs, rows, rows), F32),
            pltpu.VMEM((rows, rows), BF16),
            pltpu.VMEM((rows, rows), BF16),
            pltpu.VMEM((dim, rows), BF16),
            pltpu.VMEM((2, slots * tok, dim), F32),
            pltpu.VMEM((2, slots * tok, dim), BF16),
            pltpu.VMEM((4 * tok, dim), BF16),
            dma, dma, dma((3, 4)), dma((CHUNKS,)), dma((CHUNKS,)), dma((CHUNKS,)), dma((CHUNKS,)), dma, dma,
            dma((2, kinds, 4)), dma((2, slots)), dma((4,)), dma((4,)), dma((4,)), dma((4,)),
            dma((4,)), dma((4,)), dma((2, slots)), dma((2, kinds, 4)),
        ],
        compiler_params=pltpu.CompilerParams(
            collective_id=0, has_side_effects=True, vmem_limit_bytes=56 * 1024 * 1024
        ),
        cost_estimate=pl.CostEstimate(
            flops=5 * 10 * rows * rows * dim + 2 * tok * width * feats * 4,
            bytes_accessed=2 * (w_out.size + 8 * tok * width), transcendentals=5 * rows * rows,
        ),
    )(queries, keys, values, out_grad, w_out, offsets)
    steps = 2
    flat = pl.BlockSpec((tok // steps, width), lambda i: (i, 0))
    return pl.pallas_call(
        functools.partial(add_kernel, n, group),
        grid=(steps,),
        out_shape=(out, out, out),
        in_specs=[
            pl.BlockSpec((4, tok // steps, dim), lambda i: (0, i, 0)),
            pl.BlockSpec((2, kinds, 4, tok // steps, dim), lambda i: (0, 0, 0, i, 0)),
        ],
        out_specs=(flat, flat, flat),
        compiler_params=pltpu.CompilerParams(vmem_limit_bytes=60 * 1024 * 1024),
    )(dq_raw, parts)


def solution(mesh):
    return jax.shard_map(
        local,
        mesh=mesh,
        in_specs=(
            P("ctx", "tp"),
            P("ctx", "tp"),
            P("ctx", "tp"),
            P("ctx", "tp"),
            P("tp", None),
            P("tp", None),
        ),
        out_specs=(P("ctx", "tp"), P("ctx", "tp"), P("ctx", "tp")),
        check_vma=False,
    )
```

```python
import functools
import math

import jax
import jax.numpy as jnp
from jax import lax
from jax.experimental import pallas as pl
from jax.experimental.pallas import tpu as pltpu
from jax.sharding import PartitionSpec as P

LEVELS = 3
KEYS_SEG = 1024
MESH = pl.DeviceIdType.MESH
NEGATIVE_FILL = -1e30
CHUNKS = 4
SUB = 256
F32 = jnp.float32
BF16 = jnp.bfloat16


def nt(a, b):
    return lax.dot_general(a, b, (((1,), (1,)), ((), ())), preferred_element_type=F32)


def tn(a, b):
    return lax.dot_general(a, b, (((0,), (0,)), ((), ())), preferred_element_type=F32)


def owner_turns(group, wide, own_slot):
    turns = group // 4
    listed = [(turns, turns - 1, own_slot < group, own_slot)]
    for j in range(1, turns):
        listed.append((j, j - 1, own_slot <= 4 * j + 1, own_slot))
    if wide:
        listed.append((0, turns, own_slot < 2, group + own_slot))
    return listed


def kernel(
    n, q_ref, k_ref, v_ref, og_ref, w_hbm, off_ref, dq_ref, part_buf,
    w_buf, og_buf, stage, grad_buf, q_buf, g_buf, kv_buf, s_buf, p_buf, ds_buf, wl_buf, turned_buf,
    dkv_acc, dkv_low, dq_low,
    w_sem, og_sem, stage_sem, og_send, og_recv, fw_send, fw_recv, pair_send, pair_recv,
    kv_send, kv_recv, q_send, q_recv, g_send, g_recv,
    dq_send, dq_recv, part_send, part_recv,
):
    tok, width = q_ref.shape
    heads = off_ref.shape[0]
    dim = width // heads
    feats = og_ref.shape[1]
    group = min(KEYS_SEG * 2 ** (LEVELS - 1), tok * n) // tok
    pairs = group // 2
    rows = 2 * tok
    quads = n // 4
    turns = group // 4
    wide = n > group
    me = lax.axis_index("ctx")
    tp = lax.axis_index("tp")
    quad, head = me // 4, me % 4
    start = (4 * quad) % group
    straddle = start == 0
    u_block = (me + n - 2) % n
    own_group, own_slot = u_block // group, u_block % group
    first_group = ((4 * quad + n - 2) % n) // group
    core_peer = tp + 1 - 2 * (tp % 2)
    y_peer = (tp + 2) % 4
    far_peer = (core_peer + 2) % 4

    def move(src, dst, send, recv, target):
        @pl.when(target != me)
        def _():
            pltpu.make_async_remote_copy(
                src_ref=src, dst_ref=dst, send_sem=send, recv_sem=recv,
                device_id={"ctx": target}, device_id_type=MESH,
            ).start()

        @pl.when(target == me)
        def _():
            pltpu.make_async_copy(src, dst, recv).start()

    def sent(src, send, target):
        @pl.when(target != me)
        def _():
            pltpu.make_async_copy(src, src, send).wait()

    def arrived(dst, recv):
        pltpu.make_async_copy(dst, dst, recv).wait()

    def block(index, size):
        return pl.ds(pl.multiple_of(index * size, size), size)

    staged = []
    for kind, ref in enumerate((k_ref, v_ref, q_ref)):
        for h in range(4):
            staged.append(pltpu.make_async_copy(
                ref.at[:, pl.ds(h * dim, dim)], stage.at[kind, h], stage_sem.at[kind, h]
            ))
            staged[-1].start()
    w_copy = pltpu.make_async_copy(w_hbm, w_buf, w_sem)
    w_copy.start()
    og_copy = pltpu.make_async_copy(og_ref, og_buf.at[3], og_sem)
    og_copy.start()

    barrier = pltpu.get_barrier_semaphore()
    for step in range(1, n):
        pl.semaphore_signal(
            barrier, inc=1, device_id={"ctx": (me + step) % n}, device_id_type=MESH
        )
    for peer in (core_peer, y_peer):
        pl.semaphore_signal(barrier, inc=1, device_id={"tp": peer}, device_id_type=MESH)
    pl.semaphore_wait(barrier, n + 1)

    def tp_copy(src, dst, send, recv, peer):
        return pltpu.make_async_remote_copy(
            src_ref=src, dst_ref=dst, send_sem=send, recv_sem=recv,
            device_id={"tp": peer}, device_id_type=MESH,
        )

    piece = feats // CHUNKS
    for c in range(CHUNKS):
        part = pl.ds(c * piece, piece)
        tp_copy(
            og_ref.at[:, part], og_buf.at[1, :, part], og_send.at[c], og_recv.at[c], y_peer
        ).start()
    tp_copy(og_ref, og_buf.at[0], pair_send, pair_recv, core_peer).start()

    for copy in staged:
        copy.wait()
    turn_list = owner_turns(group, wide, own_slot)

    def send_kv(act, kind, entry):
        j, at, needed, slot = entry

        @pl.when(needed)
        def _():
            to_quad = (own_group * turns + j) % quads
            for h in range(4):
                act(kind, at, h, slot, 4 * to_quad + h)

    def start_kv(kind, at, h, slot, target):
        move(
            stage.at[kind, h], kv_buf.at[kind, block(slot, tok)],
            kv_send.at[kind, at, h], kv_recv.at[kind, slot], target,
        )

    send_kv(start_kv, 0, turn_list[0])
    for h in range(4):
        move(
            stage.at[2, h], q_buf.at[block(head, tok)],
            q_send.at[h], q_recv.at[head], 4 * quad + h,
        )
    for entry in turn_list[1:]:
        send_kv(start_kv, 0, entry)
    send_kv(start_kv, 1, turn_list[0])

    dkv_acc[...] = jnp.zeros_like(dkv_acc)

    w_copy.wait()
    og_copy.wait()

    def w_part(shard, c):
        return w_buf[:, pl.ds(pl.multiple_of(shard * feats + c * piece, piece), piece)]

    total = nt(w_buf[:, block(tp, feats)], og_buf[3])
    arrived(og_buf.at[0], pair_recv)
    total += nt(w_buf[:, block(core_peer, feats)], og_buf[0])
    for c in range(CHUNKS):
        part = pl.ds(c * piece, piece)
        arrived(og_buf.at[1, :, part], og_recv.at[c])
        tp_copy(
            og_buf.at[1, :, part], og_buf.at[2, :, part], fw_send.at[c], fw_recv.at[c], core_peer
        ).start()
        total += nt(w_part(y_peer, c), og_buf[1, :, part])
    for c in range(CHUNKS):
        part = pl.ds(c * piece, piece)
        arrived(og_buf.at[2, :, part], fw_recv.at[c])
        total += nt(w_part(far_peer, c), og_buf[2, :, part])
    for h in range(4):
        grad_buf[h] = total[h * dim:(h + 1) * dim, :].T.astype(BF16)
        move(
            grad_buf.at[h], g_buf.at[block(head, tok)],
            g_send.at[h], g_recv.at[head], 4 * quad + h,
        )

    for entry in turn_list[1:]:
        send_kv(start_kv, 1, entry)

    def wait_pair(kind, pair):
        for b in range(2):
            slot = 2 * pair + b
            arrived(kv_buf.at[kind, block(slot, tok)], kv_recv.at[kind, slot])

    for b in range(4):
        arrived(q_buf.at[block(b, tok)], q_recv.at[b])

    odd1, odd2 = off_ref[head, 1], off_ref[head, 2]
    key_row = lax.broadcasted_iota(jnp.int32, (8, rows), 0)
    query_col = lax.broadcasted_iota(jnp.int32, (8, rows), 1)
    both1 = ((key_row % 2 == odd1) & (query_col % 2 == odd1)).astype(F32)
    both2 = ((key_row % 4 == odd2) & (query_col % 4 == odd2)).astype(F32)
    sub_row = lax.broadcasted_iota(jnp.int32, (SUB, rows), 0)
    sub_col = lax.broadcasted_iota(jnp.int32, (SUB, rows), 1)
    score_scale = 1.0 / math.sqrt(dim)
    to_exp2 = score_scale / math.log(2.0)
    first_pair = jnp.where(straddle, 0, start // 2 - 1)
    first_base = jnp.where(straddle, pairs, 0) if wide else 0
    last_pair = jnp.where(straddle, pairs - 1, start // 2)
    early = jnp.where(straddle, 1, 0)
    halves = [(early, first_pair, first_base), (1 - early, last_pair, 0)]

    def arrival(turn, step):
        return step if turn == 0 else jnp.where(straddle, step, last_pair - 1 - step)

    def wait_new(turn, kind, kp):
        if turn == 0:
            wait_pair(kind, first_base + kp)
        else:
            fresh = kp > first_pair
            if wide:
                fresh = fresh | straddle
            pl.when(fresh)(functools.partial(wait_pair, kind, kp))

    def folded(values):
        return values.reshape(values.shape[0] // 8, 8, values.shape[1])

    logs = []
    for turn, (half, at_pair, base) in enumerate(halves):
        queries = q_buf[block(half, rows), :]

        turned_buf[turn] = queries.T

        def score_tile(kp, state, causal, turn=turn, at_pair=at_pair, base=base, queries=queries):
            wait_new(turn, 0, kp)
            same0 = jnp.where(at_pair // 2 == kp // 2, 1.0, 0.0)
            same1 = jnp.where(at_pair // 4 == kp // 4, 1.0, 0.0)
            count = same0 + same1 * both1 + both2
            bias = jnp.where(
                count > 2.5, math.log2(3.0),
                jnp.where(count > 1.5, 1.0, jnp.where(count > 0.5, 0.0, NEGATIVE_FILL)),
            )
            top, den = state
            for s in range(rows // SUB):
                keys = kv_buf[0, pl.ds(pl.multiple_of((base + kp) * rows + s * SUB, SUB), SUB), :]
                scores = folded(jnp.dot(keys, turned_buf[turn], preferred_element_type=F32) * to_exp2) + bias[None]
                if causal:
                    scores = scores.reshape(SUB, rows)
                    scores = folded(jnp.where(sub_row + s * SUB <= sub_col, scores, NEGATIVE_FILL))
                s_buf[turn, kp, s * SUB:(s + 1) * SUB, :] = scores.reshape(SUB, rows)
                new_top = jnp.maximum(top, jnp.max(scores, axis=0))
                den = den * jnp.exp2(top - new_top) + jnp.sum(
                    jnp.exp2(scores - new_top[None]), axis=0
                )
                top = new_top
            return top, den

        state = (jnp.full((8, rows), NEGATIVE_FILL, F32), jnp.zeros((8, rows), F32))
        state = score_tile(at_pair, state, True)
        top, den = lax.fori_loop(
            0, at_pair,
            lambda step, state, turn=turn, tile=score_tile: tile(arrival(turn, step), state, False),
            state,
        )
        row_top = jnp.max(top, axis=0, keepdims=True)
        row_total = jnp.sum(den * jnp.exp2(top - row_top), axis=0, keepdims=True)
        logs.append(row_top + jnp.log2(row_total))

    part_at = jnp.where(straddle, turns, start // 4) - 1

    def slot_owner(slot):
        return (first_group * group + slot + 2) % n

    def send_slot(kind, slot, owner, at):
        move(
            dkv_low.at[kind, block(slot, tok)], part_buf.at[kind, at, head],
            part_send.at[kind, slot], part_recv.at[kind, at, head], owner,
        )

    def round_pair(kind, kp):
        done = dkv_acc[kind, block(kp, rows), :]
        if kind == 0:
            done = done * score_scale
        dkv_low[kind, block(kp, rows), :] = done.astype(BF16)

    def send_pair(kind, kp):
        round_pair(kind, kp)
        for b in range(2):
            slot = 2 * kp + b
            send_slot(kind, slot, slot_owner(slot), part_at)

    def leaving(turn, step):
        if turn == 0:
            return step
        return (step + jnp.where(straddle, 1, 0)) % (halves[1][1] + 1)

    zero = jnp.zeros((8, rows), F32)
    bodies = []
    for turn, (half, at_pair, base) in enumerate(halves):
        for b in range(2):
            arrived(g_buf.at[block(2 * half + b, tok)], g_recv.at[2 * half + b])
        queries = q_buf[block(half, rows), :]
        grads = g_buf[block(half, rows), :]

        turned_buf[turn] = grads.T

        def weigh_body(step, num, turn=turn, base=base, grads=grads):
            kp = leaving(turn, step)
            for s in range(rows // SUB):
                here = slice(s * SUB, (s + 1) * SUB)
                weight = jnp.exp2(s_buf[turn, kp, here, :] - logs[turn])
                s_buf[turn, kp, here, :] = weight
                wl_buf[here, :] = weight.astype(BF16)
            place = block(base + kp, rows)
            dkv_acc[1, place, :] += jnp.dot(wl_buf[...], grads, preferred_element_type=F32)
            if turn == 1:
                send_pair(1, kp)
            wait_new(turn, 1, kp)
            for s in range(rows // SUB):
                here = slice(s * SUB, (s + 1) * SUB)
                vals = kv_buf[1, pl.ds(pl.multiple_of((base + kp) * rows + s * SUB, SUB), SUB), :]
                prob = jnp.dot(vals, turned_buf[turn], preferred_element_type=F32)
                p_buf[turn, kp, here, :] = prob
                num = num + jnp.sum(folded(s_buf[turn, kp, here, :] * prob), axis=0)
            return num

        bodies.append(weigh_body)

    ahead = jnp.where(straddle, pairs - 2, 0)
    num_last = lax.fori_loop(0, ahead, bodies[1], zero)
    num_first = lax.fori_loop(0, first_pair + 1, bodies[0], zero)
    num_last = lax.fori_loop(ahead, last_pair + 1, bodies[1], num_last)
    nums = (num_first, num_last)

    for turn, (half, at_pair, base) in enumerate(halves):
        queries = q_buf[block(half, rows), :]
        delta = jnp.sum(nums[turn], axis=0, keepdims=True)

        def grad_body(step, total, turn=turn, base=base, queries=queries, delta=delta):
            kp = leaving(turn, step)
            for s in range(rows // SUB):
                here = slice(s * SUB, (s + 1) * SUB)
                ds_buf[here, :] = (
                    s_buf[turn, kp, here, :] * (p_buf[turn, kp, here, :] - delta)
                ).astype(BF16)
            place = block(base + kp, rows)
            score_grad = ds_buf[...]
            dkv_acc[0, place, :] += jnp.dot(score_grad, queries, preferred_element_type=F32)
            if turn == 1:
                send_pair(0, kp)
            return total + tn(kv_buf[0, place, :], score_grad)

        total = lax.fori_loop(0, at_pair + 1, grad_body, jnp.zeros((dim, rows), F32))
        dq_low[block(half, rows), :] = (total * score_scale).T.astype(BF16)
        for b in range(2):
            move(
                dq_low.at[block(2 * half + b, tok)], dq_ref.at[head],
                dq_send.at[2 * half + b], dq_recv.at[head], 4 * quad + 2 * half + b,
            )
    if wide:
        @pl.when(straddle)
        def _():
            for kind in range(2):
                round_pair(kind, pairs)
                for b in range(2):
                    send_slot(kind, group + b, (4 * quad + b + 2) % n, turns)

    for j, at, needed, slot in turn_list:
        @pl.when(needed)
        def _(at=at):
            for kind in range(2):
                for h in range(4):
                    arrived(part_buf.at[kind, at, h], part_recv.at[kind, at, h])
    for h in range(4):
        arrived(dq_ref.at[h], dq_recv.at[h])

    for c in range(CHUNKS):
        part = pl.ds(c * piece, piece)
        pltpu.make_async_copy(og_ref.at[:, part], og_ref.at[:, part], og_send.at[c]).wait()
        pltpu.make_async_copy(og_ref.at[:, part], og_ref.at[:, part], fw_send.at[c]).wait()
    pltpu.make_async_copy(og_ref, og_ref, pair_send).wait()
    for h in range(4):
        sent(stage.at[2, h], q_send.at[h], 4 * quad + h)
        sent(grad_buf.at[h], g_send.at[h], 4 * quad + h)
        sent(dq_low.at[pl.ds(h * tok, tok)], dq_send.at[h], 4 * quad + h)

    def kv_sent(kind, at, h, slot, target):
        sent(stage.at[kind, h], kv_send.at[kind, at, h], target)

    for kind in range(2):
        for entry in turn_list:
            send_kv(kv_sent, kind, entry)

    def slot_sent(slot):
        owner = slot_owner(slot) if slot < group else (4 * quad + slot - group + 2) % n
        for kind in range(2):
            sent(dkv_low.at[kind, pl.ds(slot * tok, tok)], part_send.at[kind, slot], owner)

    for slot in range(group + 2 * wide):
        needed = straddle | (slot <= start + 1) if slot < group else straddle
        pl.when(needed)(functools.partial(slot_sent, slot))


def add_kernel(n, group, dq_ref, part_ref, dq_out, dk_out, dv_out):
    own_slot = ((lax.axis_index("ctx") + n - 2) % n) % group
    dim = dq_ref.shape[2]
    for h in range(4):
        here = slice(h * dim, (h + 1) * dim)
        dq_out[:, here] = dq_ref[h]
        for kind, out in ((0, dk_out), (1, dv_out)):
            total = None
            for j, at, needed, slot in owner_turns(group, n > group, own_slot):
                part = part_ref[kind, at, h].astype(F32)
                total = part if total is None else total + jnp.where(needed, part, 0.0)
            out[:, here] = total.astype(BF16)


def local(queries, keys, values, out_grad, w_out, offsets):
    n = lax.axis_size("ctx")
    tok, width = queries.shape
    heads = offsets.shape[0]
    dim = width // heads
    feats = out_grad.shape[1]
    group = min(KEYS_SEG * 2 ** (LEVELS - 1), tok * n) // tok
    assert heads == 4 and tok * 4 == KEYS_SEG and lax.axis_size("tp") == 4
    assert n % group == 0 and group % 4 == 0
    pairs, rows, turns = group // 2, 2 * tok, group // 4
    wide = n > group
    slots = group + 2 * wide
    kinds = turns + wide
    dma = pltpu.SemaphoreType.DMA
    out = jax.ShapeDtypeStruct((tok, width), BF16)
    hbm = pl.BlockSpec(memory_space=pl.ANY)
    dq_raw, parts = pl.pallas_call(
        functools.partial(kernel, n),
        out_shape=(
            jax.ShapeDtypeStruct((4, tok, dim), BF16),
            jax.ShapeDtypeStruct((2, kinds, 4, tok, dim), BF16),
        ),
        in_specs=[hbm] * 5 + [pl.BlockSpec(memory_space=pltpu.SMEM)],
        out_specs=(hbm, hbm),
        scratch_shapes=[
            pltpu.VMEM(w_out.shape, BF16),
            pltpu.VMEM((4, tok, feats), BF16),
            pltpu.VMEM((3, 4, tok, dim), BF16),
            pltpu.VMEM((4, tok, dim), BF16),
            pltpu.VMEM((4 * tok, dim), BF16),
            pltpu.VMEM((4 * tok, dim), BF16),
            pltpu.VMEM((2, slots * tok, dim), BF16),
            pltpu.VMEM((2, pairs, rows, rows), F32),
            pltpu.VMEM((2, pairs, rows, rows), F32),
            pltpu.VMEM((rows, rows), BF16),
            pltpu.VMEM((rows, rows), BF16),
            pltpu.VMEM((2, dim, rows), BF16),
            pltpu.VMEM((2, slots * tok, dim), F32),
            pltpu.VMEM((2, slots * tok, dim), BF16),
            pltpu.VMEM((4 * tok, dim), BF16),
            dma, dma, dma((3, 4)), dma((CHUNKS,)), dma((CHUNKS,)), dma((CHUNKS,)), dma((CHUNKS,)), dma, dma,
            dma((2, kinds, 4)), dma((2, slots)), dma((4,)), dma((4,)), dma((4,)), dma((4,)),
            dma((4,)), dma((4,)), dma((2, slots)), dma((2, kinds, 4)),
        ],
        compiler_params=pltpu.CompilerParams(
            collective_id=0, has_side_effects=True, vmem_limit_bytes=56 * 1024 * 1024
        ),
        cost_estimate=pl.CostEstimate(
            flops=5 * 10 * rows * rows * dim + 2 * tok * width * feats * 4,
            bytes_accessed=2 * (w_out.size + 8 * tok * width), transcendentals=5 * rows * rows,
        ),
    )(queries, keys, values, out_grad, w_out, offsets)
    steps = 2
    flat = pl.BlockSpec((tok // steps, width), lambda i: (i, 0))
    return pl.pallas_call(
        functools.partial(add_kernel, n, group),
        grid=(steps,),
        out_shape=(out, out, out),
        in_specs=[
            pl.BlockSpec((4, tok // steps, dim), lambda i: (0, i, 0)),
            pl.BlockSpec((2, kinds, 4, tok // steps, dim), lambda i: (0, 0, 0, i, 0)),
        ],
        out_specs=(flat, flat, flat),
        compiler_params=pltpu.CompilerParams(vmem_limit_bytes=60 * 1024 * 1024),
    )(dq_raw, parts)


def solution(mesh):
    return jax.shard_map(
        local,
        mesh=mesh,
        in_specs=(
            P("ctx", "tp"),
            P("ctx", "tp"),
            P("ctx", "tp"),
            P("ctx", "tp"),
            P("tp", None),
            P("tp", None),
        ),
        out_specs=(P("ctx", "tp"), P("ctx", "tp"), P("ctx", "tp")),
        check_vma=False,
    )
```

```python
import functools
import math

import jax
import jax.numpy as jnp
from jax import lax
from jax.experimental import pallas as pl
from jax.experimental.pallas import tpu as pltpu
from jax.sharding import PartitionSpec as P

LEVELS = 3
KEYS_SEG = 1024
MESH = pl.DeviceIdType.MESH
NEGATIVE_FILL = -1e30
CHUNKS = 4
SUB = 256
F32 = jnp.float32
BF16 = jnp.bfloat16


def nt(a, b):
    return lax.dot_general(a, b, (((1,), (1,)), ((), ())), preferred_element_type=F32)


def tn(a, b):
    return lax.dot_general(a, b, (((0,), (0,)), ((), ())), preferred_element_type=F32)


def owner_turns(group, wide, own_slot):
    turns = group // 4
    listed = [(turns, turns - 1, own_slot < group, own_slot)]
    for j in range(1, turns):
        listed.append((j, j - 1, own_slot <= 4 * j + 1, own_slot))
    if wide:
        listed.append((0, turns, own_slot < 2, group + own_slot))
    return listed


def kernel(
    n, q_ref, k_ref, v_ref, og_ref, w_hbm, off_ref, dq_ref, part_buf,
    w_buf, og_buf, stage, grad_buf, q_buf, g_buf, kv_buf, s_buf, p_buf, ds_buf, wl_buf, turned_buf,
    dkv_acc, dkv_low, dq_low,
    w_sem, og_sem, stage_sem, og_send, og_recv, fw_send, fw_recv, pair_send, pair_recv,
    kv_send, kv_recv, q_send, q_recv, g_send, g_recv,
    dq_send, dq_recv, part_send, part_recv,
):
    tok, width = q_ref.shape
    heads = off_ref.shape[0]
    dim = width // heads
    feats = og_ref.shape[1]
    group = min(KEYS_SEG * 2 ** (LEVELS - 1), tok * n) // tok
    pairs = group // 2
    rows = 2 * tok
    quads = n // 4
    turns = group // 4
    wide = n > group
    me = lax.axis_index("ctx")
    tp = lax.axis_index("tp")
    quad, head = me // 4, me % 4
    start = (4 * quad) % group
    straddle = start == 0
    u_block = (me + n - 2) % n
    own_group, own_slot = u_block // group, u_block % group
    first_group = ((4 * quad + n - 2) % n) // group
    core_peer = tp + 1 - 2 * (tp % 2)
    y_peer = (tp + 2) % 4
    far_peer = (core_peer + 2) % 4

    def move(src, dst, send, recv, target):
        @pl.when(target != me)
        def _():
            pltpu.make_async_remote_copy(
                src_ref=src, dst_ref=dst, send_sem=send, recv_sem=recv,
                device_id={"ctx": target}, device_id_type=MESH,
            ).start()

        @pl.when(target == me)
        def _():
            pltpu.make_async_copy(src, dst, recv).start()

    def sent(src, send, target):
        @pl.when(target != me)
        def _():
            pltpu.make_async_copy(src, src, send).wait()

    def arrived(dst, recv):
        pltpu.make_async_copy(dst, dst, recv).wait()

    def block(index, size):
        return pl.ds(pl.multiple_of(index * size, size), size)

    staged = []
    for kind, ref in enumerate((k_ref, v_ref, q_ref)):
        for h in range(4):
            staged.append(pltpu.make_async_copy(
                ref.at[:, pl.ds(h * dim, dim)], stage.at[kind, h], stage_sem.at[kind, h]
            ))
            staged[-1].start()
    w_copy = pltpu.make_async_copy(w_hbm, w_buf, w_sem)
    w_copy.start()
    og_copy = pltpu.make_async_copy(og_ref, og_buf.at[3], og_sem)
    og_copy.start()

    barrier = pltpu.get_barrier_semaphore()
    for step in range(1, n):
        pl.semaphore_signal(
            barrier, inc=1, device_id={"ctx": (me + step) % n}, device_id_type=MESH
        )
    for peer in (core_peer, y_peer):
        pl.semaphore_signal(barrier, inc=1, device_id={"tp": peer}, device_id_type=MESH)
    pl.semaphore_wait(barrier, n + 1)

    def tp_copy(src, dst, send, recv, peer):
        return pltpu.make_async_remote_copy(
            src_ref=src, dst_ref=dst, send_sem=send, recv_sem=recv,
            device_id={"tp": peer}, device_id_type=MESH,
        )

    piece = feats // CHUNKS
    for c in range(CHUNKS):
        part = pl.ds(c * piece, piece)
        tp_copy(
            og_ref.at[:, part], og_buf.at[1, :, part], og_send.at[c], og_recv.at[c], y_peer
        ).start()
    tp_copy(og_ref, og_buf.at[0], pair_send, pair_recv, core_peer).start()

    for copy in staged:
        copy.wait()
    turn_list = owner_turns(group, wide, own_slot)

    def send_kv(act, kind, entry):
        j, at, needed, slot = entry

        @pl.when(needed)
        def _():
            to_quad = (own_group * turns + j) % quads
            for h in range(4):
                act(kind, at, h, slot, 4 * to_quad + h)

    def start_kv(kind, at, h, slot, target):
        move(
            stage.at[kind, h], kv_buf.at[kind, block(slot, tok)],
            kv_send.at[kind, at, h], kv_recv.at[kind, slot], target,
        )

    send_kv(start_kv, 0, turn_list[0])
    for h in range(4):
        move(
            stage.at[2, h], q_buf.at[block(head, tok)],
            q_send.at[h], q_recv.at[head], 4 * quad + h,
        )
    for entry in turn_list[1:]:
        send_kv(start_kv, 0, entry)
    send_kv(start_kv, 1, turn_list[0])

    dkv_acc[...] = jnp.zeros_like(dkv_acc)

    w_copy.wait()
    og_copy.wait()

    def w_part(shard, c):
        return w_buf[:, pl.ds(pl.multiple_of(shard * feats + c * piece, piece), piece)]

    total = nt(w_buf[:, block(tp, feats)], og_buf[3])
    arrived(og_buf.at[0], pair_recv)
    total += nt(w_buf[:, block(core_peer, feats)], og_buf[0])
    def wait_pair(kind, pair):
        for b in range(2):
            slot = 2 * pair + b
            arrived(kv_buf.at[kind, block(slot, tok)], kv_recv.at[kind, slot])

    for b in range(4):
        arrived(q_buf.at[block(b, tok)], q_recv.at[b])

    odd1, odd2 = off_ref[head, 1], off_ref[head, 2]
    key_row = lax.broadcasted_iota(jnp.int32, (8, rows), 0)
    query_col = lax.broadcasted_iota(jnp.int32, (8, rows), 1)
    both1 = ((key_row % 2 == odd1) & (query_col % 2 == odd1)).astype(F32)
    both2 = ((key_row % 4 == odd2) & (query_col % 4 == odd2)).astype(F32)
    sub_row = lax.broadcasted_iota(jnp.int32, (SUB, rows), 0)
    sub_col = lax.broadcasted_iota(jnp.int32, (SUB, rows), 1)
    score_scale = 1.0 / math.sqrt(dim)
    to_exp2 = score_scale / math.log(2.0)
    first_pair = jnp.where(straddle, 0, start // 2 - 1)
    first_base = jnp.where(straddle, pairs, 0) if wide else 0
    last_pair = jnp.where(straddle, pairs - 1, start // 2)
    early = jnp.where(straddle, 1, 0)
    halves = [(early, first_pair, first_base), (1 - early, last_pair, 0)]

    def arrival(turn, step):
        return step if turn == 0 else jnp.where(straddle, step, last_pair - 1 - step)

    def wait_new(turn, kind, kp):
        if turn == 0:
            wait_pair(kind, first_base + kp)
        else:
            fresh = kp > first_pair
            if wide:
                fresh = fresh | straddle
            pl.when(fresh)(functools.partial(wait_pair, kind, kp))

    def folded(values):
        return values.reshape(values.shape[0] // 8, 8, values.shape[1])

    logs = []
    for turn, (half, at_pair, base) in enumerate(halves):
        queries = q_buf[block(half, rows), :]

        turned_buf[turn] = queries.T

        def score_tile(kp, state, causal, turn=turn, at_pair=at_pair, base=base, queries=queries):
            wait_new(turn, 0, kp)
            same0 = jnp.where(at_pair // 2 == kp // 2, 1.0, 0.0)
            same1 = jnp.where(at_pair // 4 == kp // 4, 1.0, 0.0)
            count = same0 + same1 * both1 + both2
            bias = jnp.where(
                count > 2.5, math.log2(3.0),
                jnp.where(count > 1.5, 1.0, jnp.where(count > 0.5, 0.0, NEGATIVE_FILL)),
            )
            top, den = state
            for s in range(rows // SUB):
                keys = kv_buf[0, pl.ds(pl.multiple_of((base + kp) * rows + s * SUB, SUB), SUB), :]
                scores = folded(jnp.dot(keys, turned_buf[turn], preferred_element_type=F32) * to_exp2) + bias[None]
                if causal:
                    scores = scores.reshape(SUB, rows)
                    scores = folded(jnp.where(sub_row + s * SUB <= sub_col, scores, NEGATIVE_FILL))
                s_buf[turn, kp, s * SUB:(s + 1) * SUB, :] = scores.reshape(SUB, rows)
                new_top = jnp.maximum(top, jnp.max(scores, axis=0))
                den = den * jnp.exp2(top - new_top) + jnp.sum(
                    jnp.exp2(scores - new_top[None]), axis=0
                )
                top = new_top
            return top, den

        state = (jnp.full((8, rows), NEGATIVE_FILL, F32), jnp.zeros((8, rows), F32))
        state = score_tile(at_pair, state, True)
        top, den = lax.fori_loop(
            0, at_pair,
            lambda step, state, turn=turn, tile=score_tile: tile(arrival(turn, step), state, False),
            state,
        )
        row_top = jnp.max(top, axis=0, keepdims=True)
        row_total = jnp.sum(den * jnp.exp2(top - row_top), axis=0, keepdims=True)
        logs.append(row_top + jnp.log2(row_total))

    for c in range(CHUNKS):
        part = pl.ds(c * piece, piece)
        arrived(og_buf.at[1, :, part], og_recv.at[c])
        tp_copy(
            og_buf.at[1, :, part], og_buf.at[2, :, part], fw_send.at[c], fw_recv.at[c], core_peer
        ).start()
        total += nt(w_part(y_peer, c), og_buf[1, :, part])
    for c in range(CHUNKS):
        part = pl.ds(c * piece, piece)
        arrived(og_buf.at[2, :, part], fw_recv.at[c])
        total += nt(w_part(far_peer, c), og_buf[2, :, part])
    for h in range(4):
        grad_buf[h] = total[h * dim:(h + 1) * dim, :].T.astype(BF16)
        move(
            grad_buf.at[h], g_buf.at[block(head, tok)],
            g_send.at[h], g_recv.at[head], 4 * quad + h,
        )

    for entry in turn_list[1:]:
        send_kv(start_kv, 1, entry)

    part_at = jnp.where(straddle, turns, start // 4) - 1

    def slot_owner(slot):
        return (first_group * group + slot + 2) % n

    def send_slot(kind, slot, owner, at):
        move(
            dkv_low.at[kind, block(slot, tok)], part_buf.at[kind, at, head],
            part_send.at[kind, slot], part_recv.at[kind, at, head], owner,
        )

    def round_pair(kind, kp):
        done = dkv_acc[kind, block(kp, rows), :]
        if kind == 0:
            done = done * score_scale
        dkv_low[kind, block(kp, rows), :] = done.astype(BF16)

    def send_pair(kind, kp):
        round_pair(kind, kp)
        for b in range(2):
            slot = 2 * kp + b
            send_slot(kind, slot, slot_owner(slot), part_at)

    def leaving(turn, step):
        if turn == 0:
            return step
        return (step + jnp.where(straddle, 1, 0)) % (halves[1][1] + 1)

    zero = jnp.zeros((8, rows), F32)
    bodies = []
    for turn, (half, at_pair, base) in enumerate(halves):
        for b in range(2):
            arrived(g_buf.at[block(2 * half + b, tok)], g_recv.at[2 * half + b])
        queries = q_buf[block(half, rows), :]
        grads = g_buf[block(half, rows), :]

        turned_buf[turn] = grads.T

        def weigh_body(step, num, turn=turn, base=base, grads=grads):
            kp = leaving(turn, step)
            for s in range(rows // SUB):
                here = slice(s * SUB, (s + 1) * SUB)
                weight = jnp.exp2(s_buf[turn, kp, here, :] - logs[turn])
                s_buf[turn, kp, here, :] = weight
                wl_buf[here, :] = weight.astype(BF16)
            place = block(base + kp, rows)
            dkv_acc[1, place, :] += jnp.dot(wl_buf[...], grads, preferred_element_type=F32)
            if turn == 1:
                send_pair(1, kp)
            wait_new(turn, 1, kp)
            for s in range(rows // SUB):
                here = slice(s * SUB, (s + 1) * SUB)
                vals = kv_buf[1, pl.ds(pl.multiple_of((base + kp) * rows + s * SUB, SUB), SUB), :]
                prob = jnp.dot(vals, turned_buf[turn], preferred_element_type=F32)
                p_buf[turn, kp, here, :] = prob
                num = num + jnp.sum(folded(s_buf[turn, kp, here, :] * prob), axis=0)
            return num

        bodies.append(weigh_body)

    ahead = jnp.where(straddle, pairs - 2, 0)
    num_last = lax.fori_loop(0, ahead, bodies[1], zero)
    num_first = lax.fori_loop(0, first_pair + 1, bodies[0], zero)
    num_last = lax.fori_loop(ahead, last_pair + 1, bodies[1], num_last)
    nums = (num_first, num_last)

    for turn, (half, at_pair, base) in enumerate(halves):
        queries = q_buf[block(half, rows), :]
        delta = jnp.sum(nums[turn], axis=0, keepdims=True)

        def grad_body(step, total, turn=turn, base=base, queries=queries, delta=delta):
            kp = leaving(turn, step)
            for s in range(rows // SUB):
                here = slice(s * SUB, (s + 1) * SUB)
                ds_buf[here, :] = (
                    s_buf[turn, kp, here, :] * (p_buf[turn, kp, here, :] - delta)
                ).astype(BF16)
            place = block(base + kp, rows)
            score_grad = ds_buf[...]
            dkv_acc[0, place, :] += jnp.dot(score_grad, queries, preferred_element_type=F32)
            if turn == 1:
                send_pair(0, kp)
            return total + tn(kv_buf[0, place, :], score_grad)

        total = lax.fori_loop(0, at_pair + 1, grad_body, jnp.zeros((dim, rows), F32))
        dq_low[block(half, rows), :] = (total * score_scale).T.astype(BF16)
        for b in range(2):
            move(
                dq_low.at[block(2 * half + b, tok)], dq_ref.at[head],
                dq_send.at[2 * half + b], dq_recv.at[head], 4 * quad + 2 * half + b,
            )
    if wide:
        @pl.when(straddle)
        def _():
            for kind in range(2):
                round_pair(kind, pairs)
                for b in range(2):
                    send_slot(kind, group + b, (4 * quad + b + 2) % n, turns)

    for j, at, needed, slot in turn_list:
        @pl.when(needed)
        def _(at=at):
            for kind in range(2):
                for h in range(4):
                    arrived(part_buf.at[kind, at, h], part_recv.at[kind, at, h])
    for h in range(4):
        arrived(dq_ref.at[h], dq_recv.at[h])

    for c in range(CHUNKS):
        part = pl.ds(c * piece, piece)
        pltpu.make_async_copy(og_ref.at[:, part], og_ref.at[:, part], og_send.at[c]).wait()
        pltpu.make_async_copy(og_ref.at[:, part], og_ref.at[:, part], fw_send.at[c]).wait()
    pltpu.make_async_copy(og_ref, og_ref, pair_send).wait()
    for h in range(4):
        sent(stage.at[2, h], q_send.at[h], 4 * quad + h)
        sent(grad_buf.at[h], g_send.at[h], 4 * quad + h)
        sent(dq_low.at[pl.ds(h * tok, tok)], dq_send.at[h], 4 * quad + h)

    def kv_sent(kind, at, h, slot, target):
        sent(stage.at[kind, h], kv_send.at[kind, at, h], target)

    for kind in range(2):
        for entry in turn_list:
            send_kv(kv_sent, kind, entry)

    def slot_sent(slot):
        owner = slot_owner(slot) if slot < group else (4 * quad + slot - group + 2) % n
        for kind in range(2):
            sent(dkv_low.at[kind, pl.ds(slot * tok, tok)], part_send.at[kind, slot], owner)

    for slot in range(group + 2 * wide):
        needed = straddle | (slot <= start + 1) if slot < group else straddle
        pl.when(needed)(functools.partial(slot_sent, slot))


def add_kernel(n, group, dq_ref, part_ref, dq_out, dk_out, dv_out):
    own_slot = ((lax.axis_index("ctx") + n - 2) % n) % group
    dim = dq_ref.shape[2]
    for h in range(4):
        here = slice(h * dim, (h + 1) * dim)
        dq_out[:, here] = dq_ref[h]
        for kind, out in ((0, dk_out), (1, dv_out)):
            total = None
            for j, at, needed, slot in owner_turns(group, n > group, own_slot):
                part = part_ref[kind, at, h].astype(F32)
                total = part if total is None else total + jnp.where(needed, part, 0.0)
            out[:, here] = total.astype(BF16)


def local(queries, keys, values, out_grad, w_out, offsets):
    n = lax.axis_size("ctx")
    tok, width = queries.shape
    heads = offsets.shape[0]
    dim = width // heads
    feats = out_grad.shape[1]
    group = min(KEYS_SEG * 2 ** (LEVELS - 1), tok * n) // tok
    assert heads == 4 and tok * 4 == KEYS_SEG and lax.axis_size("tp") == 4
    assert n % group == 0 and group % 4 == 0
    pairs, rows, turns = group // 2, 2 * tok, group // 4
    wide = n > group
    slots = group + 2 * wide
    kinds = turns + wide
    dma = pltpu.SemaphoreType.DMA
    out = jax.ShapeDtypeStruct((tok, width), BF16)
    hbm = pl.BlockSpec(memory_space=pl.ANY)
    dq_raw, parts = pl.pallas_call(
        functools.partial(kernel, n),
        out_shape=(
            jax.ShapeDtypeStruct((4, tok, dim), BF16),
            jax.ShapeDtypeStruct((2, kinds, 4, tok, dim), BF16),
        ),
        in_specs=[hbm] * 5 + [pl.BlockSpec(memory_space=pltpu.SMEM)],
        out_specs=(hbm, hbm),
        scratch_shapes=[
            pltpu.VMEM(w_out.shape, BF16),
            pltpu.VMEM((4, tok, feats), BF16),
            pltpu.VMEM((3, 4, tok, dim), BF16),
            pltpu.VMEM((4, tok, dim), BF16),
            pltpu.VMEM((4 * tok, dim), BF16),
            pltpu.VMEM((4 * tok, dim), BF16),
            pltpu.VMEM((2, slots * tok, dim), BF16),
            pltpu.VMEM((2, pairs, rows, rows), F32),
            pltpu.VMEM((2, pairs, rows, rows), F32),
            pltpu.VMEM((rows, rows), BF16),
            pltpu.VMEM((rows, rows), BF16),
            pltpu.VMEM((2, dim, rows), BF16),
            pltpu.VMEM((2, slots * tok, dim), F32),
            pltpu.VMEM((2, slots * tok, dim), BF16),
            pltpu.VMEM((4 * tok, dim), BF16),
            dma, dma, dma((3, 4)), dma((CHUNKS,)), dma((CHUNKS,)), dma((CHUNKS,)), dma((CHUNKS,)), dma, dma,
            dma((2, kinds, 4)), dma((2, slots)), dma((4,)), dma((4,)), dma((4,)), dma((4,)),
            dma((4,)), dma((4,)), dma((2, slots)), dma((2, kinds, 4)),
        ],
        compiler_params=pltpu.CompilerParams(
            collective_id=0, has_side_effects=True, vmem_limit_bytes=56 * 1024 * 1024
        ),
        cost_estimate=pl.CostEstimate(
            flops=5 * 10 * rows * rows * dim + 2 * tok * width * feats * 4,
            bytes_accessed=2 * (w_out.size + 8 * tok * width), transcendentals=5 * rows * rows,
        ),
    )(queries, keys, values, out_grad, w_out, offsets)
    steps = 2
    flat = pl.BlockSpec((tok // steps, width), lambda i: (i, 0))
    return pl.pallas_call(
        functools.partial(add_kernel, n, group),
        grid=(steps,),
        out_shape=(out, out, out),
        in_specs=[
            pl.BlockSpec((4, tok // steps, dim), lambda i: (0, i, 0)),
            pl.BlockSpec((2, kinds, 4, tok // steps, dim), lambda i: (0, 0, 0, i, 0)),
        ],
        out_specs=(flat, flat, flat),
        compiler_params=pltpu.CompilerParams(vmem_limit_bytes=60 * 1024 * 1024),
    )(dq_raw, parts)


def solution(mesh):
    return jax.shard_map(
        local,
        mesh=mesh,
        in_specs=(
            P("ctx", "tp"),
            P("ctx", "tp"),
            P("ctx", "tp"),
            P("ctx", "tp"),
            P("tp", None),
            P("tp", None),
        ),
        out_specs=(P("ctx", "tp"), P("ctx", "tp"), P("ctx", "tp")),
        check_vma=False,
    )
```
